32 devices in a mesh: pb: 4 (over y, x), ka: 8 (over z, core).
Axes of the slice: x: 2, y: 2, z: 4, core: 2. Of those that a mesh axis runs over, the one named last changes fastest.
Arguments:
- queries: bfloat16 [4096, 2048], P(('pb', 'ka')), may hold values from -3 to 3
- keys: bfloat16 [4096, 2048], P(('pb', 'ka')), may hold values from -3 to 3
- values: bfloat16 [4096, 2048], P(('pb', 'ka')), may hold values from -3 to 3
- outputs: bfloat16 [4096, 2048], P(('pb', 'ka')), may hold values from -3 to 3
- d_out: bfloat16 [4096, 2048], P(('pb', 'ka')), may hold values from -16 to 16
- row_lse: float32 [16, 4096], P(None, ('pb', 'ka')), may hold values from 6.5 to 8.5
- adjacency: int32 [32, 2, 4, 1], P(('pb', 'ka')), may hold values from 0 to 1, as said below
Outputs:
- grad_queries: bfloat16 [4096, 2048], P(('pb', 'ka'))
- grad_keys: bfloat16 [4096, 2048], P(('pb', 'ka'))
- grad_values: bfloat16 [4096, 2048], P(('pb', 'ka'))
The draws below stay inside these ranges and needn't reach their ends.
Inputs may be any that keep to these rules, and one draw needn't show every extreme that they name: 1 where the query block attends that key block of its window, else 0; every query block attends its own key block, adjacency[b, 0, 0, 0] = 1.
All inputs are finite; a program needn't handle non-finite values.
Results may differ from the reference program's by a relative error of at most 0.0075.
Values may be sent and summed in bfloat16 or wider, within the bound.
A program may use at most 128 MiB of HBM per device.

```python
import math
import jax
import jax.numpy as jnp
from jax import lax

HEADS = 16
HEAD_DIM = 128
BLOCK = 128
WINDOW = 4
TOK_DEV = 128
D = 2048
BLOCKS_DEV = 1
GRID_ROWS = 4
GRID_COLS = 8
TOKENS = 4096
QBLOCKS = 32


def draw_adjacency(key, part):
    level_key = jax.random.fold_in(key, 11)
    entry_key = jax.random.fold_in(key, 23)
    device_total = GRID_ROWS * GRID_COLS
    levels = jax.random.randint(level_key, (device_total,), 0, 4)
    shift_amount = jnp.where(levels == 0, 0, levels + 1).astype(jnp.int32)
    limits = jnp.right_shift(jnp.full((device_total,), 16, jnp.int32), shift_amount)
    per_block = jnp.repeat(limits, BLOCKS_DEV, total_repeat_length=QBLOCKS)
    rolls = jax.random.randint(entry_key, (QBLOCKS, 2, WINDOW, BLOCKS_DEV), 0, 16)
    present = rolls < per_block[:, None, None, None]
    block_ids = jnp.arange(QBLOCKS, dtype=jnp.int32) % BLOCKS_DEV
    row_ids = jnp.arange(2, dtype=jnp.int32)
    col_ids = jnp.arange(WINDOW, dtype=jnp.int32)
    key_ids = jnp.arange(BLOCKS_DEV, dtype=jnp.int32)
    own_block = (row_ids[None, :, None, None] == 0) & (col_ids[None, None, :, None] == 0) & (key_ids[None, None, None, :] == block_ids[:, None, None, None])
    return (present | own_block).astype(jnp.int32)


def shard_levels(key, extent, pieces, least, largest):
    loudness, own = 1.0, jax.random.fold_in(key, 6)
    for position, shards_of in pieces:
        draws = jnp.exp(jax.random.uniform(jax.random.fold_in(own, position), (shards_of,), jnp.float32, least / len(pieces), largest / len(pieces)))
        loudness = loudness * jnp.repeat(draws, extent[position] // shards_of).reshape([-1 if axis == position else 1 for axis in range(len(extent))])
    return loudness


def gaussian(key, shape, scale, limit, cuts=(), kind=jnp.bfloat16):
    drawn = jax.random.normal(key, shape, jnp.float32) * scale
    if len(cuts) > 0:
        drawn = shard_levels(key, shape, cuts, -0.22, 0.18) * drawn
    return jnp.clip(drawn, min=-limit, max=limit).astype(kind)


def setup_inputs(seed: int = 0) -> dict:
    seeds = jax.random.split(jax.random.key(seed), 8)
    queries = gaussian(seeds[0], (TOKENS, D), 1.0, 3.0, ((0, 32),))
    keys = gaussian(seeds[1], (TOKENS, D), 1.0, 3.0, ((0, 32),))
    values = gaussian(seeds[2], (TOKENS, D), 1.0, 3.0, ((0, 32),))
    outputs = gaussian(seeds[3], (TOKENS, D), 1.0, 3.0, ((0, 32),))
    d_out = gaussian(seeds[4], (TOKENS, D), 6.0, 16.0, ((0, 32),))
    row_lse = jnp.clip(6.5 + 2.0 * jax.random.uniform(seeds[5], (HEADS, TOKENS), jnp.float32) ** shard_levels(seeds[5], (HEADS, TOKENS), ((1, 32),), -0.2, 0.2), 6.5, 8.5)
    adjacency = draw_adjacency(jax.random.fold_in(seeds[7], 71), 0)
    return dict(queries=queries, keys=keys, values=values, outputs=outputs, d_out=d_out, row_lse=row_lse, adjacency=adjacency)


def spread_mask(block_mask):
    block_count = block_mask.shape[0]
    full = jnp.broadcast_to(block_mask[:, None, :, None], (block_count, BLOCK, block_count, BLOCK))
    return full.reshape(block_count * BLOCK, block_count * BLOCK)

def pair_terms(query_rows, grad_rows, row_norms, row_delta, key_rows, value_rows, allowed):
    inverse = 1.0 / math.sqrt(HEAD_DIM)
    query_heads = query_rows.astype(jnp.float32).reshape(TOK_DEV, HEADS, HEAD_DIM)
    grad_heads = grad_rows.astype(jnp.float32).reshape(TOK_DEV, HEADS, HEAD_DIM)
    key_heads = key_rows.astype(jnp.float32).reshape(TOK_DEV, HEADS, HEAD_DIM)
    value_heads = value_rows.astype(jnp.float32).reshape(TOK_DEV, HEADS, HEAD_DIM)
    scores = jnp.einsum('ihe,the->hit', query_heads, key_heads) * inverse
    prob_full = jnp.where(allowed[None], jnp.exp(scores - row_norms[:, :, None]), jnp.float32(0.0))
    prob_low = lax.optimization_barrier(prob_full.astype(jnp.bfloat16)).astype(jnp.float32)
    prob_grad = jnp.einsum('ihe,the->hit', grad_heads, value_heads)
    score_grad = (prob_full * (prob_grad - row_delta[:, :, None]) * inverse).astype(jnp.bfloat16)
    score_grad = lax.optimization_barrier(score_grad).astype(jnp.float32)
    grad_v = jnp.einsum('hit,ihe->the', prob_low, grad_heads).reshape(TOK_DEV, D)
    grad_q = jnp.einsum('hit,the->ihe', score_grad, key_heads).reshape(TOK_DEV, D)
    grad_k = jnp.einsum('hit,ihe->the', score_grad, query_heads).reshape(TOK_DEV, D)
    return (grad_q, grad_k, grad_v)

def add_rows(total, start, term):
    current = lax.dynamic_slice_in_dim(total, start, TOK_DEV, 0)
    return lax.dynamic_update_slice_in_dim(total, current + term, start, 0)

def reference(queries, keys, values, outputs, d_out, row_lse, adjacency):
    product = d_out.astype(jnp.float32) * outputs.astype(jnp.float32)
    delta_all = lax.optimization_barrier(jnp.sum(product.reshape(TOKENS, HEADS, HEAD_DIM), axis=2)).T

    def per_device(totals, device_index):
        grad_keys, grad_values = totals
        grid_row = device_index // GRID_COLS
        grid_col = device_index % GRID_COLS
        start = (device_index * TOK_DEV).astype(jnp.int32)
        query_rows = lax.dynamic_slice_in_dim(queries, start, TOK_DEV, 0)
        grad_rows = lax.dynamic_slice_in_dim(d_out, start, TOK_DEV, 0)
        row_norms = lax.dynamic_slice_in_dim(row_lse, start, TOK_DEV, 1)
        row_delta = lax.dynamic_slice_in_dim(delta_all, start, TOK_DEV, 1)
        blocks = lax.dynamic_slice_in_dim(adjacency, (device_index * BLOCKS_DEV).astype(jnp.int32), BLOCKS_DEV, 0)
        grad_query = jnp.zeros((TOK_DEV, D), jnp.float32)
        for row_step in range(2):
            for col_step in range(WINDOW):
                key_device = (grid_row + row_step) % GRID_ROWS * GRID_COLS + (grid_col + col_step) % GRID_COLS
                key_start = (key_device * TOK_DEV).astype(jnp.int32)
                key_rows = lax.dynamic_slice_in_dim(keys, key_start, TOK_DEV, 0)
                value_rows = lax.dynamic_slice_in_dim(values, key_start, TOK_DEV, 0)
                allowed = spread_mask(blocks[:, row_step, col_step, :] == 1)
                term_q, term_k, term_v = pair_terms(query_rows, grad_rows, row_norms, row_delta, key_rows, value_rows, allowed)
                grad_query = grad_query + term_q
                grad_keys = add_rows(grad_keys, key_start, term_k)
                grad_values = add_rows(grad_values, key_start, term_v)
        return ((grad_keys, grad_values), grad_query.astype(jnp.bfloat16))
    empty_rows = jnp.zeros((TOKENS, D), jnp.float32)
    device_list = jnp.arange(GRID_ROWS * GRID_COLS, dtype=jnp.int32)
    (grad_keys, grad_values), grad_blocks = lax.scan(per_device, (empty_rows, empty_rows), device_list)
    grad_queries = grad_blocks.reshape(TOKENS, D)
    return (grad_queries, grad_keys.astype(jnp.bfloat16), grad_values.astype(jnp.bfloat16))
```

```python
import functools
import math

import jax
import jax.numpy as jnp
from jax import lax
from jax.experimental import pallas as pl
from jax.experimental.pallas import tpu as pltpu
from jax.sharding import PartitionSpec as P

HEAD_DIM = 128
BLOCK = 128
WINDOW = 4
GROUP_HEADS = 2
BIG = 1e30
MESH = pl.DeviceIdType.MESH

Q1, Q2, Q3, KV, R3, R2, R1, GKV = range(8)
KINDS = 8


def dot(a, b, da, db):
    return lax.dot_general(a, b, (((da,), (db,)), ((), ())), preferred_element_type=jnp.float32)


def kernel(
    rows, cols, groups, heads,
    q_ref, k_ref, v_ref, o_ref, do_ref, lse_ref, adj_ref,
    gq_out, gk_out, gv_out,
    visit, kvb, stats, gq_part, gkv_near, gq_send, gq_recv, gkv_send, gkv_recv,
    send_sem, recv_sem, stat_send, stat_recv,
):
    inverse = 1.0 / math.sqrt(HEAD_DIM)
    width = GROUP_HEADS * HEAD_DIM
    r = lax.axis_index("pb")
    c = lax.axis_index("ka")
    right = (r, lax.rem(c + 1, cols))
    left = (r, lax.rem(c + cols - 1, cols))
    below = (lax.rem(r + 1, rows), c)
    above = (lax.rem(r + rows - 1, rows), c)

    barrier = pltpu.get_barrier_semaphore()
    for other in (right, left, below, above):
        pl.semaphore_signal(barrier, inc=1, device_id=other, device_id_type=MESH)
    pl.semaphore_wait(barrier, 4)

    def message(kind, g):
        if kind in (Q1, Q2, Q3):
            src, dst, to = visit.at[kind, g], visit.at[kind + 1, g], right
        elif kind == KV:
            src = kvb.at[g, :, pl.ds(0, BLOCK), :]
            dst = kvb.at[g, :, pl.ds(BLOCK, BLOCK), :]
            to = above
        elif kind == GKV:
            src, dst, to = gkv_send.at[g], gkv_recv.at[g], below
        else:
            src, dst, to = gq_send.at[kind - R3, g], gq_recv.at[kind - R3, g], left
        return pltpu.make_async_remote_copy(
            src_ref=src, dst_ref=dst,
            send_sem=send_sem.at[kind, g], recv_sem=recv_sem.at[kind, g],
            device_id=to, device_id_type=MESH,
        )

    def stat_message(w):
        return pltpu.make_async_remote_copy(
            src_ref=stats.at[w], dst_ref=stats.at[w + 1],
            send_sem=stat_send.at[w], recv_sem=stat_recv.at[w],
            device_id=right, device_id_type=MESH,
        )

    def columns(g):
        return pl.ds(pl.multiple_of(g * width, width), width)

    def begin(g):
        here = columns(g)
        visit[0, g, 0] = q_ref[:, here]
        visit[0, g, 1] = do_ref[:, here]
        message(Q1, g).start()
        kvb[g, 0, pl.ds(0, BLOCK), :] = k_ref[:, here]
        kvb[g, 1, pl.ds(0, BLOCK), :] = v_ref[:, here]
        message(KV, g).start()

    def make_stats():
        ones = jnp.ones((8, HEAD_DIM), jnp.bfloat16)
        stats[0, pl.ds(0, heads), :] = lse_ref[...]
        for h in range(heads):
            part = pl.ds(h * HEAD_DIM, HEAD_DIM)
            product = do_ref[:, part].astype(jnp.float32) * o_ref[:, part].astype(jnp.float32)
            high = product.astype(jnp.bfloat16)
            low = (product - high.astype(jnp.float32)).astype(jnp.bfloat16)
            delta = dot(ones, high, 1, 1) + dot(ones, low, 1, 1)
            stats[0, pl.ds(heads + h, 1), :] = delta[0:1]
        for a in range(2):
            for w in range(WINDOW):
                blocked = (1 - adj_ref[0, a, w, 0]).astype(jnp.float32) * BIG
                stats[0, pl.ds(2 * heads + a * WINDOW + w, 1), :] = jnp.full((1, BLOCK), blocked, jnp.float32)

    def compute(g):
        for hh in range(GROUP_HEADS):
            h = g * GROUP_HEADS + hh
            part = slice(hh * HEAD_DIM, (hh + 1) * HEAD_DIM)
            kk = kvb[g, 0, :, part]
            vv = kvb[g, 1, :, part]
            qq = jnp.concatenate([visit[w, g, 0, :, part] for w in range(WINDOW)], axis=0)
            dd = jnp.concatenate([visit[w, g, 1, :, part] for w in range(WINDOW)], axis=0)
            delta = jnp.concatenate(
                [stats[w, pl.ds(heads + h, 1), :] for w in range(WINDOW)], axis=1
            )
            norms = [
                jnp.concatenate(
                    [
                        stats[w, pl.ds(h, 1), :] + stats[w, pl.ds(2 * heads + a * WINDOW + w, 1), :]
                        for w in range(WINDOW)
                    ],
                    axis=1,
                )
                for a in range(2)
            ]
            scores = dot(kk, qq, 1, 1) * inverse
            prob = jnp.concatenate(
                [jnp.exp(scores[:BLOCK] - norms[0]), jnp.exp(scores[BLOCK:] - norms[1])], axis=0
            )
            prob_grad = dot(vv, dd, 1, 1)
            score_grad = (prob * (prob_grad - delta) * inverse).astype(jnp.bfloat16)
            grad_v = dot(prob.astype(jnp.bfloat16), dd, 1, 0)
            grad_k = dot(score_grad, qq, 1, 0)
            grad_q = dot(score_grad, kk, 0, 0)
            gkv_near[g, 0, :, part] = grad_k[:BLOCK]
            gkv_near[g, 1, :, part] = grad_v[:BLOCK]
            gkv_send[g, 0, :, part] = grad_k[BLOCK:].astype(jnp.bfloat16)
            gkv_send[g, 1, :, part] = grad_v[BLOCK:].astype(jnp.bfloat16)
            for w in range(WINDOW - 1):
                gq_part[w, g, :, part] = grad_q[w * BLOCK : (w + 1) * BLOCK]
            gq_send[0, g, :, part] = grad_q[(WINDOW - 1) * BLOCK :].astype(jnp.bfloat16)

    def add_on(kind, g):
        step = kind - R3
        message(kind - 1, g).wait_recv()
        total = gq_recv[step - 1, g].astype(jnp.float32) + gq_part[WINDOW - 1 - step, g]
        gq_send[step, g] = total.astype(jnp.bfloat16)
        message(kind, g).start()

    def finish(g):
        here = columns(g)
        message(R1, g).wait_recv()
        total = gq_recv[2, g].astype(jnp.float32) + gq_part[0, g]
        gq_out[:, here] = total.astype(jnp.bfloat16)
        message(GKV, g).wait_recv()
        gk_out[:, here] = (gkv_near[g, 0] + gkv_recv[g, 0].astype(jnp.float32)).astype(jnp.bfloat16)
        gv_out[:, here] = (gkv_near[g, 1] + gkv_recv[g, 1].astype(jnp.float32)).astype(jnp.bfloat16)

    def at(i, skew, action):
        g = i - skew

        @pl.when((g >= 0) & (g < groups))
        def _():
            action(g)

    def forward(kind, g):
        message(kind - 1, g).wait_recv()
        message(kind, g).start()

    def work(g):
        message(Q3, g).wait_recv()
        message(KV, g).wait_recv()
        compute(g)
        message(R3, g).start()
        message(GKV, g).start()

    def turn(i, carry):
        at(i, 0, begin)

        @pl.when(i == 0)
        def _():
            make_stats()
            stat_message(0).start()

        for w in (1, 2):

            @pl.when(i == w)
            def _():
                stat_message(w - 1).wait_recv()
                stat_message(w).start()

        at(i, 1, functools.partial(forward, Q2))
        at(i, 2, functools.partial(forward, Q3))

        @pl.when(i == 3)
        def _():
            stat_message(2).wait_recv()

        at(i, 3, work)
        at(i, 4, functools.partial(add_on, R2))
        at(i, 5, functools.partial(add_on, R1))
        at(i, 6, finish)
        return carry

    lax.fori_loop(0, groups + 6, turn, 0)

    for w in range(WINDOW - 1):
        stat_message(w).wait_send()

    def drain(g, carry):
        for kind in range(KINDS):
            message(kind, g).wait_send()
        return carry

    lax.fori_loop(0, groups, drain, 0)


def local(rows, cols, queries, keys, values, outputs, d_out, row_lse, adjacency):
    tokens, features = queries.shape
    heads = features // HEAD_DIM
    groups = heads // GROUP_HEADS
    width = GROUP_HEADS * HEAD_DIM
    low, wide = jnp.bfloat16, jnp.float32
    vmem = pl.BlockSpec(memory_space=pltpu.VMEM)
    out = jax.ShapeDtypeStruct((tokens, features), low)
    pairs = 2 * WINDOW * heads
    return pl.pallas_call(
        functools.partial(kernel, rows, cols, groups, heads),
        out_shape=(out, out, out),
        in_specs=[vmem] * 6 + [pl.BlockSpec(memory_space=pltpu.SMEM)],
        out_specs=(vmem, vmem, vmem),
        scratch_shapes=[
            pltpu.VMEM((WINDOW, groups, 2, BLOCK, width), low),
            pltpu.VMEM((groups, 2, 2 * BLOCK, width), low),
            pltpu.VMEM((WINDOW, 2 * heads + 2 * WINDOW, BLOCK), wide),
            pltpu.VMEM((WINDOW - 1, groups, BLOCK, width), wide),
            pltpu.VMEM((groups, 2, BLOCK, width), wide),
            pltpu.VMEM((WINDOW - 1, groups, BLOCK, width), low),
            pltpu.VMEM((WINDOW - 1, groups, BLOCK, width), low),
            pltpu.VMEM((groups, 2, BLOCK, width), low),
            pltpu.VMEM((groups, 2, BLOCK, width), low),
            pltpu.SemaphoreType.DMA((KINDS, groups)),
            pltpu.SemaphoreType.DMA((KINDS, groups)),
            pltpu.SemaphoreType.DMA((WINDOW - 1,)),
            pltpu.SemaphoreType.DMA((WINDOW - 1,)),
        ],
        compiler_params=pltpu.CompilerParams(
            collective_id=0, has_side_effects=True, vmem_limit_bytes=48 * 1024 * 1024
        ),
        cost_estimate=pl.CostEstimate(
            flops=pairs * 5 * 2 * BLOCK * BLOCK * HEAD_DIM,
            bytes_accessed=8 * tokens * features * 2,
            transcendentals=pairs * BLOCK * BLOCK,
        ),
        name="block_sparse_backward",
    )(queries, keys, values, outputs, d_out, row_lse, adjacency)


def solution(mesh):
    token_rows = P(("pb", "ka"), None)
    placed = (token_rows,) * 5 + (P(None, ("pb", "ka")), P(("pb", "ka"), None, None, None))
    return jax.shard_map(
        functools.partial(local, mesh.shape["pb"], mesh.shape["ka"]),
        mesh=mesh,
        in_specs=placed,
        out_specs=(token_rows, token_rows, token_rows),
        check_vma=False,
    )
```

```python
import functools
import math

import jax
import jax.numpy as jnp
from jax import lax
from jax.experimental import pallas as pl
from jax.experimental.pallas import tpu as pltpu
from jax.sharding import PartitionSpec as P

HEAD_DIM = 128
BLOCK = 128
WINDOW = 4
GROUP_HEADS = 1
AHEAD = 4
BIG = 1e30
MESH = pl.DeviceIdType.MESH

Q1, Q2, Q3, KV, R3, R2, R1, GKV = range(8)
KINDS = 8


def dot(a, b, da, db):
    return lax.dot_general(a, b, (((da,), (db,)), ((), ())), preferred_element_type=jnp.float32)


def kernel(
    rows, cols, groups, heads,
    q_hbm, k_hbm, v_hbm, o_hbm, do_hbm, lse_hbm, adj_ref,
    gq_out, gk_out, gv_out,
    q_ref, k_ref, v_ref, o_ref, do_ref, lse_ref, load_sem, done, done_sem,
    visit, kvb, stats, gq_part, gkv_near, gq_send, gq_recv, gkv_send, gkv_recv,
    send_sem, recv_sem, stat_send, stat_recv,
):
    inverse = 1.0 / math.sqrt(HEAD_DIM)
    width = GROUP_HEADS * HEAD_DIM
    r = lax.axis_index("pb")
    c = lax.axis_index("ka")
    right = (r, lax.rem(c + 1, cols))
    left = (r, lax.rem(c + cols - 1, cols))
    below = (lax.rem(r + 1, rows), c)
    above = (lax.rem(r + rows - 1, rows), c)

    loads = [
        pltpu.make_async_copy(source, target, load_sem.at[n])
        for n, (source, target) in enumerate(
            (
                (q_hbm, q_ref),
                (do_hbm, do_ref),
                (k_hbm, k_ref),
                (v_hbm, v_ref),
                (o_hbm, o_ref),
                (lse_hbm, lse_ref),
            )
        )
    ]
    for load in loads:
        load.start()

    barrier = pltpu.get_barrier_semaphore()
    for other in (right, left, below, above):
        pl.semaphore_signal(barrier, inc=1, device_id=other, device_id_type=MESH)
    pl.semaphore_wait(barrier, 4)

    def message(kind, g):
        if kind in (Q1, Q2, Q3):
            src, dst, to = visit.at[kind, g], visit.at[kind + 1, g], right
        elif kind == KV:
            src = kvb.at[g, :, pl.ds(0, BLOCK), :]
            dst = kvb.at[g, :, pl.ds(BLOCK, BLOCK), :]
            to = above
        elif kind == GKV:
            src, dst, to = gkv_send.at[g], gkv_recv.at[g], below
        else:
            src, dst, to = gq_send.at[kind - R3, g], gq_recv.at[kind - R3, g], left
        return pltpu.make_async_remote_copy(
            src_ref=src, dst_ref=dst,
            send_sem=send_sem.at[kind, g], recv_sem=recv_sem.at[kind, g],
            device_id=to, device_id_type=MESH,
        )

    def stat_message(w):
        return pltpu.make_async_remote_copy(
            src_ref=stats.at[w], dst_ref=stats.at[w + 1],
            send_sem=stat_send.at[w], recv_sem=stat_recv.at[w],
            device_id=right, device_id_type=MESH,
        )

    def columns(g):
        return pl.ds(pl.multiple_of(g * width, width), width)

    def begin(g):
        here = columns(g)
        visit[0, g, 0] = q_ref[:, here]
        visit[0, g, 1] = do_ref[:, here]
        message(Q1, g).start()
        kvb[g, 0, pl.ds(0, BLOCK), :] = k_ref[:, here]
        kvb[g, 1, pl.ds(0, BLOCK), :] = v_ref[:, here]
        message(KV, g).start()

    def make_stats():
        ones = jnp.ones((8, HEAD_DIM), jnp.bfloat16)
        stats[0, pl.ds(0, heads), :] = lse_ref[...]
        for h in range(heads):
            part = pl.ds(h * HEAD_DIM, HEAD_DIM)
            product = do_ref[:, part].astype(jnp.float32) * o_ref[:, part].astype(jnp.float32)
            high = product.astype(jnp.bfloat16)
            low = (product - high.astype(jnp.float32)).astype(jnp.bfloat16)
            delta = dot(ones, high, 1, 1) + dot(ones, low, 1, 1)
            stats[0, pl.ds(heads + h, 1), :] = delta[0:1]
        for a in range(2):
            for w in range(WINDOW):
                blocked = (1 - adj_ref[0, a, 0, w]).astype(jnp.float32) * BIG
                stats[0, pl.ds(2 * heads + a * WINDOW + w, 1), :] = jnp.full((1, BLOCK), blocked, jnp.float32)

    def compute(g):
        for hh in range(GROUP_HEADS):
            h = g * GROUP_HEADS + hh
            part = slice(hh * HEAD_DIM, (hh + 1) * HEAD_DIM)
            kk = kvb[g, 0, :, part]
            vv = kvb[g, 1, :, part]
            qq = jnp.concatenate([visit[w, g, 0, :, part] for w in range(WINDOW)], axis=0)
            dd = jnp.concatenate([visit[w, g, 1, :, part] for w in range(WINDOW)], axis=0)
            delta = jnp.concatenate(
                [stats[w, pl.ds(heads + h, 1), :] for w in range(WINDOW)], axis=1
            )
            norms = [
                jnp.concatenate(
                    [
                        stats[w, pl.ds(h, 1), :] + stats[w, pl.ds(2 * heads + a * WINDOW + w, 1), :]
                        for w in range(WINDOW)
                    ],
                    axis=1,
                )
                for a in range(2)
            ]
            scores = dot(kk, qq, 1, 1) * inverse
            prob = jnp.concatenate(
                [jnp.exp(scores[:BLOCK] - norms[0]), jnp.exp(scores[BLOCK:] - norms[1])], axis=0
            )
            prob_grad = dot(vv, dd, 1, 1)
            score_grad = (prob * (prob_grad - delta) * inverse).astype(jnp.bfloat16)
            grad_v = dot(prob.astype(jnp.bfloat16), dd, 1, 0)
            grad_k = dot(score_grad, qq, 1, 0)
            grad_q = dot(score_grad, kk, 0, 0)
            gkv_near[g, 0, :, part] = grad_k[:BLOCK]
            gkv_near[g, 1, :, part] = grad_v[:BLOCK]
            gkv_send[g, 0, :, part] = grad_k[BLOCK:].astype(jnp.bfloat16)
            gkv_send[g, 1, :, part] = grad_v[BLOCK:].astype(jnp.bfloat16)
            for w in range(WINDOW - 1):
                gq_part[w, g, :, part] = grad_q[w * BLOCK : (w + 1) * BLOCK]
            gq_send[0, g, :, part] = grad_q[(WINDOW - 1) * BLOCK :].astype(jnp.bfloat16)

    def add_on(kind, g):
        step = kind - R3
        message(kind - 1, g).wait_recv()
        total = gq_recv[step - 1, g].astype(jnp.float32) + gq_part[WINDOW - 1 - step, g]
        gq_send[step, g] = total.astype(jnp.bfloat16)
        message(kind, g).start()

    def store(n, g):
        out = (gq_out, gk_out, gv_out)[n]
        return pltpu.make_async_copy(done.at[n, g], out.at[:, columns(g)], done_sem.at[n, g])

    def finish(g):
        message(R1, g).wait_recv()
        total = gq_recv[2, g].astype(jnp.float32) + gq_part[0, g]
        done[0, g] = total.astype(jnp.bfloat16)
        message(GKV, g).wait_recv()
        for n in range(2):
            total = gkv_near[g, n] + gkv_recv[g, n].astype(jnp.float32)
            done[n + 1, g] = total.astype(jnp.bfloat16)
        for n in range(3):
            store(n, g).start()

    def at(i, skew, action):
        g = i - skew

        @pl.when((g >= 0) & (g < groups))
        def _():
            action(g)

    def forward(kind, g):
        message(kind - 1, g).wait_recv()
        message(kind, g).start()

    def work(g):
        message(Q3, g).wait_recv()
        message(KV, g).wait_recv()
        compute(g)
        message(R3, g).start()
        message(GKV, g).start()

    def stats_forward(w):
        stat_message(w - 1).wait_recv()
        stat_message(w).start()

    def turn(i, carry):
        at(i, -AHEAD, begin)
        at(i, 0, functools.partial(forward, Q2))

        @pl.when(i == 0)
        def _():
            stats_forward(1)

        at(i, 2, functools.partial(forward, Q3))

        @pl.when(i == 2)
        def _():
            stats_forward(2)

        @pl.when(i == 4)
        def _():
            stat_message(2).wait_recv()

        at(i, 4, work)
        at(i, 6, functools.partial(add_on, R2))
        at(i, 8, functools.partial(add_on, R1))
        at(i, 10, finish)
        return carry

    for load in loads[:4]:
        load.wait()
    for g in range(AHEAD):
        begin(g)
    for load in loads[4:]:
        load.wait()
    make_stats()
    stat_message(0).start()

    lax.fori_loop(0, groups + 10, turn, 0)

    for w in range(WINDOW - 1):
        stat_message(w).wait_send()

    def drain(g, carry):
        for kind in range(KINDS):
            message(kind, g).wait_send()
        for n in range(3):
            store(n, g).wait()
        return carry

    lax.fori_loop(0, groups, drain, 0)


def store_kernel(a_ref, b_ref, c_ref, a_out, b_out, c_out, sem):
    stores = [
        pltpu.make_async_copy(source, target, sem.at[n])
        for n, (source, target) in enumerate(((a_ref, a_out), (b_ref, b_out), (c_ref, c_out)))
    ]
    for store in stores:
        store.start()
    for store in stores:
        store.wait()


def local(rows, cols, queries, keys, values, outputs, d_out, row_lse, adjacency):
    tokens, features = queries.shape
    heads = features // HEAD_DIM
    groups = heads // GROUP_HEADS
    width = GROUP_HEADS * HEAD_DIM
    low, wide = jnp.bfloat16, jnp.float32
    hbm = pl.BlockSpec(memory_space=pltpu.HBM)
    out = jax.ShapeDtypeStruct((tokens, features), low)
    pairs = 2 * WINDOW * heads
    grads = pl.pallas_call(
        functools.partial(kernel, rows, cols, groups, heads),
        out_shape=(out, out, out),
        in_specs=[hbm] * 6 + [pl.BlockSpec(memory_space=pltpu.SMEM)],
        out_specs=(hbm, hbm, hbm),
        scratch_shapes=[pltpu.VMEM((tokens, features), low)] * 5
        + [
            pltpu.VMEM((heads, tokens), wide),
            pltpu.SemaphoreType.DMA((6,)),
            pltpu.VMEM((3, groups, BLOCK, width), low),
            pltpu.SemaphoreType.DMA((3, groups)),
            pltpu.VMEM((WINDOW, groups, 2, BLOCK, width), low),
            pltpu.VMEM((groups, 2, 2 * BLOCK, width), low),
            pltpu.VMEM((WINDOW, 2 * heads + 2 * WINDOW, BLOCK), wide),
            pltpu.VMEM((WINDOW - 1, groups, BLOCK, width), wide),
            pltpu.VMEM((groups, 2, BLOCK, width), wide),
            pltpu.VMEM((WINDOW - 1, groups, BLOCK, width), low),
            pltpu.VMEM((WINDOW - 1, groups, BLOCK, width), low),
            pltpu.VMEM((groups, 2, BLOCK, width), low),
            pltpu.VMEM((groups, 2, BLOCK, width), low),
            pltpu.SemaphoreType.DMA((KINDS, groups)),
            pltpu.SemaphoreType.DMA((KINDS, groups)),
            pltpu.SemaphoreType.DMA((WINDOW - 1,)),
            pltpu.SemaphoreType.DMA((WINDOW - 1,)),
        ],
        compiler_params=pltpu.CompilerParams(
            collective_id=0, has_side_effects=True, vmem_limit_bytes=62 * 1024 * 1024
        ),
        cost_estimate=pl.CostEstimate(
            flops=pairs * 5 * 2 * BLOCK * BLOCK * HEAD_DIM,
            bytes_accessed=8 * tokens * features * 2,
            transcendentals=pairs * BLOCK * BLOCK,
        ),
        name="block_sparse_backward",
    )(queries, keys, values, outputs, d_out, row_lse, adjacency.transpose(0, 1, 3, 2))
    return pl.pallas_call(
        store_kernel,
        out_shape=(out, out, out),
        in_specs=[hbm] * 3,
        out_specs=(hbm, hbm, hbm),
        scratch_shapes=[pltpu.SemaphoreType.DMA((3,))],
        compiler_params=pltpu.CompilerParams(vmem_limit_bytes=62 * 1024 * 1024),
        name="store_gradients",
    )(*grads)


def solution(mesh):
    token_rows = P(("pb", "ka"), None)
    placed = (token_rows,) * 5 + (P(None, ("pb", "ka")), P(("pb", "ka"), None, None, None))
    return jax.shard_map(
        functools.partial(local, mesh.shape["pb"], mesh.shape["ka"]),
        mesh=mesh,
        in_specs=placed,
        out_specs=(token_rows, token_rows, token_rows),
        check_vma=False,
    )
```

```python
import functools
import math

import jax
import jax.numpy as jnp
from jax import lax
from jax.experimental import pallas as pl
from jax.experimental.pallas import tpu as pltpu
from jax.sharding import PartitionSpec as P

HEAD_DIM = 128
BLOCK = 128
WINDOW = 4
GROUP_HEADS = 1
AHEAD = 8
BIG = 1e30
MESH = pl.DeviceIdType.MESH

Q1, Q2, Q3, KV, R3, R2, R1, GKV = range(8)
KINDS = 8


def dot(a, b, da, db):
    return lax.dot_general(a, b, (((da,), (db,)), ((), ())), preferred_element_type=jnp.float32)


def kernel(
    rows, cols, groups, heads,
    q_hbm, k_hbm, v_hbm, o_hbm, do_hbm, lse_hbm, adj_ref,
    gq_out, gk_out, gv_out,
    q_ref, k_ref, v_ref, o_ref, do_ref, lse_ref, load_sem, done, done_sem,
    visit, kvb, stats, gq_part, gkv_near, gq_send, gq_recv, gkv_send, gkv_recv,
    send_sem, recv_sem, stat_send, stat_recv,
):
    inverse = 1.0 / math.sqrt(HEAD_DIM)
    width = GROUP_HEADS * HEAD_DIM
    r = lax.axis_index("pb")
    c = lax.axis_index("ka")
    right = (r, lax.rem(c + 1, cols))
    left = (r, lax.rem(c + cols - 1, cols))
    below = (lax.rem(r + 1, rows), c)
    above = (lax.rem(r + rows - 1, rows), c)

    loads = [
        pltpu.make_async_copy(source, target, load_sem.at[n])
        for n, (source, target) in enumerate(
            (
                (q_hbm, q_ref),
                (do_hbm, do_ref),
                (k_hbm, k_ref),
                (v_hbm, v_ref),
                (o_hbm, o_ref),
                (lse_hbm, lse_ref),
            )
        )
    ]
    for load in loads:
        load.start()

    barrier = pltpu.get_barrier_semaphore()
    for other in (right, left, below, above):
        pl.semaphore_signal(barrier, inc=1, device_id=other, device_id_type=MESH)
    pl.semaphore_wait(barrier, 4)

    def message(kind, g):
        if kind in (Q1, Q2, Q3):
            src, dst, to = visit.at[kind, g], visit.at[kind + 1, g], right
        elif kind == KV:
            src = kvb.at[g, :, pl.ds(0, BLOCK), :]
            dst = kvb.at[g, :, pl.ds(BLOCK, BLOCK), :]
            to = above
        elif kind == GKV:
            src, dst, to = gkv_send.at[g], gkv_recv.at[g], below
        else:
            src, dst, to = gq_send.at[kind - R3, g], gq_recv.at[kind - R3, g], left
        return pltpu.make_async_remote_copy(
            src_ref=src, dst_ref=dst,
            send_sem=send_sem.at[kind, g], recv_sem=recv_sem.at[kind, g],
            device_id=to, device_id_type=MESH,
        )

    def stat_message(w):
        return pltpu.make_async_remote_copy(
            src_ref=stats.at[w], dst_ref=stats.at[w + 1],
            send_sem=stat_send.at[w], recv_sem=stat_recv.at[w],
            device_id=right, device_id_type=MESH,
        )

    def columns(g):
        return pl.ds(pl.multiple_of(g * width, width), width)

    def begin_queries(g):
        here = columns(g)
        visit[0, g, 0] = q_ref[:, here]
        visit[0, g, 1] = do_ref[:, here]
        message(Q1, g).start()

    def begin_keys(g):
        here = columns(g)
        kvb[g, 0, pl.ds(0, BLOCK), :] = k_ref[:, here]
        kvb[g, 1, pl.ds(0, BLOCK), :] = v_ref[:, here]
        message(KV, g).start()

    def make_stats():
        ones = jnp.ones((8, HEAD_DIM), jnp.bfloat16)
        stats[0, pl.ds(0, heads), :] = lse_ref[...]
        for h in range(heads):
            part = pl.ds(h * HEAD_DIM, HEAD_DIM)
            product = do_ref[:, part].astype(jnp.float32) * o_ref[:, part].astype(jnp.float32)
            high = product.astype(jnp.bfloat16)
            low = (product - high.astype(jnp.float32)).astype(jnp.bfloat16)
            delta = dot(ones, high, 1, 1) + dot(ones, low, 1, 1)
            stats[0, pl.ds(heads + h, 1), :] = delta[0:1]
        for a in range(2):
            for w in range(WINDOW):
                blocked = (1 - adj_ref[0, a, 0, w]).astype(jnp.float32) * BIG
                stats[0, pl.ds(2 * heads + a * WINDOW + w, 1), :] = jnp.full((1, BLOCK), blocked, jnp.float32)

    def compute(g):
        for hh in range(GROUP_HEADS):
            h = g * GROUP_HEADS + hh
            part = slice(hh * HEAD_DIM, (hh + 1) * HEAD_DIM)
            kk = kvb[g, 0, :, part]
            vv = kvb[g, 1, :, part]
            qq = jnp.concatenate([visit[w, g, 0, :, part] for w in range(WINDOW)], axis=0)
            dd = jnp.concatenate([visit[w, g, 1, :, part] for w in range(WINDOW)], axis=0)
            delta = jnp.concatenate(
                [stats[w, pl.ds(heads + h, 1), :] for w in range(WINDOW)], axis=1
            )
            norms = [
                jnp.concatenate(
                    [
                        stats[w, pl.ds(h, 1), :] + stats[w, pl.ds(2 * heads + a * WINDOW + w, 1), :]
                        for w in range(WINDOW)
                    ],
                    axis=1,
                )
                for a in range(2)
            ]
            scores = dot(kk, qq, 1, 1) * inverse
            prob = jnp.concatenate(
                [jnp.exp(scores[:BLOCK] - norms[0]), jnp.exp(scores[BLOCK:] - norms[1])], axis=0
            )
            prob_grad = dot(vv, dd, 1, 1)
            score_grad = (prob * (prob_grad - delta) * inverse).astype(jnp.bfloat16)
            grad_v = dot(prob.astype(jnp.bfloat16), dd, 1, 0)
            grad_k = dot(score_grad, qq, 1, 0)
            grad_q = dot(score_grad, kk, 0, 0)
            gkv_near[g, 0, :, part] = grad_k[:BLOCK]
            gkv_near[g, 1, :, part] = grad_v[:BLOCK]
            gkv_send[g, 0, :, part] = grad_k[BLOCK:].astype(jnp.bfloat16)
            gkv_send[g, 1, :, part] = grad_v[BLOCK:].astype(jnp.bfloat16)
            for w in range(WINDOW - 1):
                gq_part[w, g, :, part] = grad_q[w * BLOCK : (w + 1) * BLOCK]
            gq_send[0, g, :, part] = grad_q[(WINDOW - 1) * BLOCK :].astype(jnp.bfloat16)

    def add_on(kind, g):
        step = kind - R3
        message(kind - 1, g).wait_recv()
        total = gq_recv[step - 1, g].astype(jnp.float32) + gq_part[WINDOW - 1 - step, g]
        gq_send[step, g] = total.astype(jnp.bfloat16)
        message(kind, g).start()

    def store(n, g):
        out = (gq_out, gk_out, gv_out)[n]
        return pltpu.make_async_copy(done.at[n, g], out.at[:, columns(g)], done_sem.at[n, g])

    def finish(g):
        message(R1, g).wait_recv()
        total = gq_recv[2, g].astype(jnp.float32) + gq_part[0, g]
        done[0, g] = total.astype(jnp.bfloat16)
        message(GKV, g).wait_recv()
        for n in range(2):
            total = gkv_near[g, n] + gkv_recv[g, n].astype(jnp.float32)
            done[n + 1, g] = total.astype(jnp.bfloat16)
        for n in range(3):
            store(n, g).start()
        for kind in range(KINDS):
            message(kind, g).wait_send()

    def settle(g):
        for n in range(3):
            store(n, g).wait()

    def at(i, skew, action):
        g = i - skew

        @pl.when((g >= 0) & (g < groups))
        def _():
            action(g)

    def forward(kind, g):
        message(kind - 1, g).wait_recv()
        message(kind, g).start()

    def work(g):
        message(Q3, g).wait_recv()
        message(KV, g).wait_recv()
        compute(g)
        message(R3, g).start()
        message(GKV, g).start()

    def stats_forward(w):
        stat_message(w - 1).wait_recv()
        stat_message(w).start()

    def turn(i, carry):
        at(i, -AHEAD, begin_queries)
        at(i, -AHEAD, begin_keys)
        at(i, 0, functools.partial(forward, Q2))

        @pl.when(i == 0)
        def _():
            stats_forward(1)

        at(i, 2, functools.partial(forward, Q3))

        @pl.when(i == 2)
        def _():
            stats_forward(2)

        @pl.when(i == 4)
        def _():
            stat_message(2).wait_recv()

        at(i, 4, work)
        at(i, 6, functools.partial(add_on, R2))
        at(i, 8, functools.partial(add_on, R1))
        at(i, 10, finish)
        at(i, 12, settle)
        return carry

    for load in loads[:2]:
        load.wait()
    for g in range(AHEAD):
        begin_queries(g)
    for load in loads[2:4]:
        load.wait()
    for g in range(AHEAD):
        begin_keys(g)
    for load in loads[4:]:
        load.wait()
    make_stats()
    stat_message(0).start()

    lax.fori_loop(0, groups + 12, turn, 0)

    for w in range(WINDOW - 1):
        stat_message(w).wait_send()


def store_kernel(a_ref, b_ref, c_ref, a_out, b_out, c_out, held, in_sem, out_sem):
    half = a_ref.shape[0] // 2
    refs = ((a_ref, a_out), (b_ref, b_out), (c_ref, c_out))
    pieces = [(n, p, pl.ds(p * half, half)) for p in range(2) for n in range(3)]
    fetches = [
        pltpu.make_async_copy(refs[n][0].at[here], held.at[n, here], in_sem.at[n, p])
        for n, p, here in pieces
    ]
    stores = [
        pltpu.make_async_copy(held.at[n, here], refs[n][1].at[here], out_sem.at[n, p])
        for n, p, here in pieces
    ]
    for fetch in fetches:
        fetch.start()
    for fetch, store in zip(fetches, stores):
        fetch.wait()
        store.start()
    for store in stores:
        store.wait()


def local(rows, cols, queries, keys, values, outputs, d_out, row_lse, adjacency):
    tokens, features = queries.shape
    heads = features // HEAD_DIM
    groups = heads // GROUP_HEADS
    width = GROUP_HEADS * HEAD_DIM
    low, wide = jnp.bfloat16, jnp.float32
    hbm = pl.BlockSpec(memory_space=pltpu.HBM)
    out = jax.ShapeDtypeStruct((tokens, features), low)
    pairs = 2 * WINDOW * heads
    grads = pl.pallas_call(
        functools.partial(kernel, rows, cols, groups, heads),
        out_shape=(out, out, out),
        in_specs=[hbm] * 6 + [pl.BlockSpec(memory_space=pltpu.SMEM)],
        out_specs=(hbm, hbm, hbm),
        scratch_shapes=[pltpu.VMEM((tokens, features), low)] * 5
        + [
            pltpu.VMEM((heads, tokens), wide),
            pltpu.SemaphoreType.DMA((6,)),
            pltpu.VMEM((3, groups, BLOCK, width), low),
            pltpu.SemaphoreType.DMA((3, groups)),
            pltpu.VMEM((WINDOW, groups, 2, BLOCK, width), low),
            pltpu.VMEM((groups, 2, 2 * BLOCK, width), low),
            pltpu.VMEM((WINDOW, 2 * heads + 2 * WINDOW, BLOCK), wide),
            pltpu.VMEM((WINDOW - 1, groups, BLOCK, width), wide),
            pltpu.VMEM((groups, 2, BLOCK, width), wide),
            pltpu.VMEM((WINDOW - 1, groups, BLOCK, width), low),
            pltpu.VMEM((WINDOW - 1, groups, BLOCK, width), low),
            pltpu.VMEM((groups, 2, BLOCK, width), low),
            pltpu.VMEM((groups, 2, BLOCK, width), low),
            pltpu.SemaphoreType.DMA((KINDS, groups)),
            pltpu.SemaphoreType.DMA((KINDS, groups)),
            pltpu.SemaphoreType.DMA((WINDOW - 1,)),
            pltpu.SemaphoreType.DMA((WINDOW - 1,)),
        ],
        compiler_params=pltpu.CompilerParams(
            collective_id=0, has_side_effects=True, vmem_limit_bytes=62 * 1024 * 1024
        ),
        cost_estimate=pl.CostEstimate(
            flops=pairs * 5 * 2 * BLOCK * BLOCK * HEAD_DIM,
            bytes_accessed=8 * tokens * features * 2,
            transcendentals=pairs * BLOCK * BLOCK,
        ),
        name="block_sparse_backward",
    )(queries, keys, values, outputs, d_out, row_lse, adjacency.transpose(0, 1, 3, 2))
    return pl.pallas_call(
        store_kernel,
        out_shape=(out, out, out),
        in_specs=[hbm] * 3,
        out_specs=(hbm, hbm, hbm),
        scratch_shapes=[
            pltpu.VMEM((3, tokens, features), low),
            pltpu.SemaphoreType.DMA((3, 2)),
            pltpu.SemaphoreType.DMA((3, 2)),
        ],
        compiler_params=pltpu.CompilerParams(vmem_limit_bytes=62 * 1024 * 1024),
        name="store_gradients",
    )(*grads)


def solution(mesh):
    token_rows = P(("pb", "ka"), None)
    placed = (token_rows,) * 5 + (P(None, ("pb", "ka")), P(("pb", "ka"), None, None, None))
    return jax.shard_map(
        functools.partial(local, mesh.shape["pb"], mesh.shape["ka"]),
        mesh=mesh,
        in_specs=placed,
        out_specs=(token_rows, token_rows, token_rows),
        check_vma=False,
    )
```

```python
import functools
import math

import jax
import jax.numpy as jnp
from jax import lax
from jax.experimental import pallas as pl
from jax.experimental.pallas import tpu as pltpu
from jax.sharding import PartitionSpec as P

HEAD_DIM = 128
BLOCK = 128
WINDOW = 4
AHEAD = 4
BIG = 1e30
MESH = pl.DeviceIdType.MESH

Q1, Q2, Q3, KV, R3, R2, R1, GKV = range(8)
KINDS = 8


def dot(a, b, da, db):
    return lax.dot_general(a, b, (((da,), (db,)), ((), ())), preferred_element_type=jnp.float32)


def kernel(
    rows, cols, groups, heads,
    q_hbm, k_hbm, v_hbm, o_hbm, do_hbm, lse_hbm, adj_ref,
    gq_out, gk_out, gv_out,
    q_ref, k_ref, v_ref, o_ref, do_ref, lse_ref, load_sem, done, done_sem,
    visit, kvb, stats, probs, score_grads, gq_part, gkv_near, gq_send, gq_recv, gkv_send, gkv_recv,
    send_sem, recv_sem, stat_send, stat_recv,
):
    inverse = 1.0 / math.sqrt(HEAD_DIM)
    width = HEAD_DIM
    r = lax.axis_index("pb")
    c = lax.axis_index("ka")
    right = (r, lax.rem(c + 1, cols))
    left = (r, lax.rem(c + cols - 1, cols))
    below = (lax.rem(r + 1, rows), c)
    above = (lax.rem(r + rows - 1, rows), c)

    loads = [
        pltpu.make_async_copy(source, target, load_sem.at[n])
        for n, (source, target) in enumerate(
            (
                (q_hbm, q_ref),
                (do_hbm, do_ref),
                (k_hbm, k_ref),
                (v_hbm, v_ref),
                (o_hbm, o_ref),
                (lse_hbm, lse_ref),
            )
        )
    ]
    for load in loads:
        load.start()

    barrier = pltpu.get_barrier_semaphore()
    for other in (right, left, below, above):
        pl.semaphore_signal(barrier, inc=1, device_id=other, device_id_type=MESH)
    pl.semaphore_wait(barrier, 4)

    def message(kind, g):
        if kind in (Q1, Q2, Q3):
            src, dst, to = visit.at[kind, g], visit.at[kind + 1, g], right
        elif kind == KV:
            src = kvb.at[g, :, pl.ds(0, BLOCK), :]
            dst = kvb.at[g, :, pl.ds(BLOCK, BLOCK), :]
            to = above
        elif kind == GKV:
            src, dst, to = gkv_send.at[g], gkv_recv.at[g], below
        else:
            src, dst, to = gq_send.at[kind - R3, g], gq_recv.at[kind - R3, g], left
        return pltpu.make_async_remote_copy(
            src_ref=src, dst_ref=dst,
            send_sem=send_sem.at[kind, g], recv_sem=recv_sem.at[kind, g],
            device_id=to, device_id_type=MESH,
        )

    def stat_message(w):
        return pltpu.make_async_remote_copy(
            src_ref=stats.at[w], dst_ref=stats.at[w + 1],
            send_sem=stat_send.at[w], recv_sem=stat_recv.at[w],
            device_id=right, device_id_type=MESH,
        )

    def columns(g):
        return pl.ds(pl.multiple_of(g * width, width), width)

    def begin_queries(g):
        here = columns(g)
        visit[0, g, 0] = q_ref[:, here]
        visit[0, g, 1] = do_ref[:, here]
        message(Q1, g).start()

    def begin_keys(g):
        here = columns(g)
        kvb[g, 0, pl.ds(0, BLOCK), :] = k_ref[:, here]
        kvb[g, 1, pl.ds(0, BLOCK), :] = v_ref[:, here]
        message(KV, g).start()

    def make_stats():
        ones = jnp.ones((8, HEAD_DIM), jnp.bfloat16)
        stats[0, pl.ds(0, heads), :] = lse_ref[...]
        for h in range(heads):
            part = pl.ds(h * HEAD_DIM, HEAD_DIM)
            product = do_ref[:, part].astype(jnp.float32) * o_ref[:, part].astype(jnp.float32)
            high = product.astype(jnp.bfloat16)
            low = (product - high.astype(jnp.float32)).astype(jnp.bfloat16)
            delta = dot(ones, high, 1, 1) + dot(ones, low, 1, 1)
            stats[0, pl.ds(heads + h, 1), :] = delta[0:1]
        for a in range(2):
            for w in range(WINDOW):
                blocked = (1 - adj_ref[0, a, 0, w]).astype(jnp.float32) * BIG
                stats[0, pl.ds(2 * heads + a * WINDOW + w, 1), :] = jnp.full((1, BLOCK), blocked, jnp.float32)

    def pair_terms(g, first):
        pair = (first, first + 1)
        span = pl.ds(first * BLOCK, 2 * BLOCK)
        kk = kvb[g, 0]
        vv = kvb[g, 1]
        qq = visit[first : first + 2, g, 0].reshape(2 * BLOCK, HEAD_DIM)
        dd = visit[first : first + 2, g, 1].reshape(2 * BLOCK, HEAD_DIM)
        delta = jnp.concatenate([stats[w, pl.ds(heads + g, 1), :] for w in pair], axis=1)
        for a in range(2):
            norms = jnp.concatenate(
                [
                    stats[w, pl.ds(g, 1), :] + stats[w, pl.ds(2 * heads + a * WINDOW + w, 1), :]
                    for w in pair
                ],
                axis=1,
            )
            half = slice(a * BLOCK, (a + 1) * BLOCK)
            prob = jnp.exp(dot(kk[half], qq, 1, 1) * inverse - norms)
            probs[g, half, span] = prob.astype(jnp.bfloat16)
            prob_grad = dot(vv[half], dd, 1, 1)
            score_grad = prob * (prob_grad - delta) * inverse
            score_grads[g, half, span] = score_grad.astype(jnp.bfloat16)
        return dot(score_grads[g, :, span], kk, 0, 0)

    def work_near(g):
        message(KV, g).wait_recv()
        grad_q = pair_terms(g, 0)
        gq_part[0, g] = grad_q[:BLOCK]
        gq_part[1, g] = grad_q[BLOCK:]

    def work_far(g):
        message(Q3, g).wait_recv()
        grad_q = pair_terms(g, 2)
        gq_part[2, g] = grad_q[:BLOCK]
        gq_send[0, g] = grad_q[BLOCK:].astype(jnp.bfloat16)
        message(R3, g).start()
        qq = visit[:, g, 0].reshape(WINDOW * BLOCK, HEAD_DIM)
        dd = visit[:, g, 1].reshape(WINDOW * BLOCK, HEAD_DIM)
        for n, total in ((0, dot(score_grads[g], qq, 1, 0)), (1, dot(probs[g], dd, 1, 0))):
            gkv_near[g, n] = total[:BLOCK]
            gkv_send[g, n] = total[BLOCK:].astype(jnp.bfloat16)
        message(GKV, g).start()

    def add_on(kind, g):
        step = kind - R3
        message(kind - 1, g).wait_recv()
        total = gq_recv[step - 1, g].astype(jnp.float32) + gq_part[WINDOW - 1 - step, g]
        gq_send[step, g] = total.astype(jnp.bfloat16)
        message(kind, g).start()

    def store(n, g):
        out = (gq_out, gk_out, gv_out)[n]
        return pltpu.make_async_copy(done.at[n, g], out.at[:, columns(g)], done_sem.at[n, g])

    def finish(g):
        message(R1, g).wait_recv()
        total = gq_recv[2, g].astype(jnp.float32) + gq_part[0, g]
        done[0, g] = total.astype(jnp.bfloat16)
        message(GKV, g).wait_recv()
        for n in range(2):
            total = gkv_near[g, n] + gkv_recv[g, n].astype(jnp.float32)
            done[n + 1, g] = total.astype(jnp.bfloat16)
        for n in range(3):
            store(n, g).start()
        for kind in range(KINDS):
            message(kind, g).wait_send()

    def settle(g):
        for n in range(3):
            store(n, g).wait()

    def at(i, skew, action):
        g = i - skew

        @pl.when((g >= 0) & (g < groups))
        def _():
            action(g)

    def forward(kind, g):
        message(kind - 1, g).wait_recv()
        message(kind, g).start()

    def stats_forward(w):
        stat_message(w - 1).wait_recv()
        stat_message(w).start()

    def turn(i, carry):
        at(i, -AHEAD, begin_queries)
        at(i, -AHEAD, begin_keys)
        at(i, 0, functools.partial(forward, Q2))

        @pl.when(i == 0)
        def _():
            stats_forward(1)

        at(i, 1, work_near)
        at(i, 2, functools.partial(forward, Q3))

        @pl.when(i == 2)
        def _():
            stats_forward(2)

        @pl.when(i == 4)
        def _():
            stat_message(2).wait_recv()

        at(i, 4, work_far)
        at(i, 6, functools.partial(add_on, R2))
        at(i, 8, functools.partial(add_on, R1))
        at(i, 10, finish)
        at(i, 12, settle)
        return carry

    for load in loads[:2]:
        load.wait()
    for g in range(AHEAD):
        begin_queries(g)
    for load in loads[2:4]:
        load.wait()
    for g in range(AHEAD):
        begin_keys(g)
    for load in loads[4:]:
        load.wait()
    make_stats()
    stat_message(0).start()

    lax.fori_loop(0, groups + 12, turn, 0)

    for w in range(WINDOW - 1):
        stat_message(w).wait_send()


def store_kernel(a_ref, b_ref, c_ref, a_out, b_out, c_out, held, in_sem, out_sem):
    half = a_ref.shape[0] // 2
    refs = ((a_ref, a_out), (b_ref, b_out), (c_ref, c_out))
    pieces = [(n, p, pl.ds(p * half, half)) for p in range(2) for n in range(3)]
    fetches = [
        pltpu.make_async_copy(refs[n][0].at[here], held.at[n, here], in_sem.at[n, p])
        for n, p, here in pieces
    ]
    stores = [
        pltpu.make_async_copy(held.at[n, here], refs[n][1].at[here], out_sem.at[n, p])
        for n, p, here in pieces
    ]
    for fetch in fetches:
        fetch.start()
    for fetch, store in zip(fetches, stores):
        fetch.wait()
        store.start()
    for store in stores:
        store.wait()


def local(rows, cols, queries, keys, values, outputs, d_out, row_lse, adjacency):
    tokens, features = queries.shape
    heads = features // HEAD_DIM
    groups = heads
    width = HEAD_DIM
    low, wide = jnp.bfloat16, jnp.float32
    hbm = pl.BlockSpec(memory_space=pltpu.HBM)
    out = jax.ShapeDtypeStruct((tokens, features), low)
    pairs = 2 * WINDOW * heads
    grads = pl.pallas_call(
        functools.partial(kernel, rows, cols, groups, heads),
        out_shape=(out, out, out),
        in_specs=[hbm] * 6 + [pl.BlockSpec(memory_space=pltpu.SMEM)],
        out_specs=(hbm, hbm, hbm),
        scratch_shapes=[pltpu.VMEM((tokens, features), low)] * 5
        + [
            pltpu.VMEM((heads, tokens), wide),
            pltpu.SemaphoreType.DMA((6,)),
            pltpu.VMEM((3, groups, BLOCK, width), low),
            pltpu.SemaphoreType.DMA((3, groups)),
            pltpu.VMEM((WINDOW, groups, 2, BLOCK, width), low),
            pltpu.VMEM((groups, 2, 2 * BLOCK, width), low),
            pltpu.VMEM((WINDOW, 2 * heads + 2 * WINDOW, BLOCK), wide),
            pltpu.VMEM((groups, 2 * BLOCK, WINDOW * BLOCK), low),
            pltpu.VMEM((groups, 2 * BLOCK, WINDOW * BLOCK), low),
            pltpu.VMEM((WINDOW - 1, groups, BLOCK, width), wide),
            pltpu.VMEM((groups, 2, BLOCK, width), wide),
            pltpu.VMEM((WINDOW - 1, groups, BLOCK, width), low),
            pltpu.VMEM((WINDOW - 1, groups, BLOCK, width), low),
            pltpu.VMEM((groups, 2, BLOCK, width), low),
            pltpu.VMEM((groups, 2, BLOCK, width), low),
            pltpu.SemaphoreType.DMA((KINDS, groups)),
            pltpu.SemaphoreType.DMA((KINDS, groups)),
            pltpu.SemaphoreType.DMA((WINDOW - 1,)),
            pltpu.SemaphoreType.DMA((WINDOW - 1,)),
        ],
        compiler_params=pltpu.CompilerParams(
            collective_id=0, has_side_effects=True, vmem_limit_bytes=62 * 1024 * 1024
        ),
        cost_estimate=pl.CostEstimate(
            flops=pairs * 5 * 2 * BLOCK * BLOCK * HEAD_DIM,
            bytes_accessed=8 * tokens * features * 2,
            transcendentals=pairs * BLOCK * BLOCK,
        ),
        name="block_sparse_backward",
    )(queries, keys, values, outputs, d_out, row_lse, adjacency.transpose(0, 1, 3, 2))
    return pl.pallas_call(
        store_kernel,
        out_shape=(out, out, out),
        in_specs=[hbm] * 3,
        out_specs=(hbm, hbm, hbm),
        scratch_shapes=[
            pltpu.VMEM((3, tokens, features), low),
            pltpu.SemaphoreType.DMA((3, 2)),
            pltpu.SemaphoreType.DMA((3, 2)),
        ],
        compiler_params=pltpu.CompilerParams(vmem_limit_bytes=62 * 1024 * 1024),
        name="store_gradients",
    )(*grads)


def solution(mesh):
    token_rows = P(("pb", "ka"), None)
    placed = (token_rows,) * 5 + (P(None, ("pb", "ka")), P(("pb", "ka"), None, None, None))
    return jax.shard_map(
        functools.partial(local, mesh.shape["pb"], mesh.shape["ka"]),
        mesh=mesh,
        in_specs=placed,
        out_specs=(token_rows, token_rows, token_rows),
        check_vma=False,
    )
```

```python
import functools
import math

import jax
import jax.numpy as jnp
from jax import lax
from jax.experimental import pallas as pl
from jax.experimental.pallas import tpu as pltpu
from jax.sharding import PartitionSpec as P

HEAD_DIM = 128
BLOCK = 128
WINDOW = 4
AHEAD = 8
BIG = 1e30
MESH = pl.DeviceIdType.MESH

Q1, Q2, Q3, KV, R3, R2, R1, GKV = range(8)
KINDS = 8


def dot(a, b, da, db):
    return lax.dot_general(a, b, (((da,), (db,)), ((), ())), preferred_element_type=jnp.float32)


def kernel(
    rows, cols, groups, heads,
    q_hbm, k_hbm, v_hbm, o_hbm, do_hbm, lse_hbm, adj_ref,
    gq_out, gk_out, gv_out,
    q_ref, k_ref, v_ref, o_ref, do_ref, lse_ref, load_sem, done, done_sem,
    visit, kvb, stats, probs, score_grads, gq_part, gkv_near, gq_send, gq_recv, gkv_send, gkv_recv,
    send_sem, recv_sem, stat_send, stat_recv, gq_leap, leap_send, leap_recv,
):
    inverse = 1.0 / math.sqrt(HEAD_DIM)
    width = HEAD_DIM
    r = lax.axis_index("pb")
    c = lax.axis_index("ka")
    right = (r, lax.rem(c + 1, cols))
    left = (r, lax.rem(c + cols - 1, cols))
    below = (lax.rem(r + 1, rows), c)
    above = (lax.rem(r + rows - 1, rows), c)
    leaps = c == cols - (WINDOW - 1)
    lands = c == 0
    skips = c == cols - 1
    leap_to = (r, 0)
    leap_from = (r, cols - (WINDOW - 1))

    ahead = pl.ds(0, AHEAD * width)
    rest = pl.ds(AHEAD * width, (groups - AHEAD) * width)
    loads = [
        pltpu.make_async_copy(source, target, load_sem.at[n])
        for n, (source, target) in enumerate(
            (
                (q_hbm.at[:, ahead], q_ref.at[:, ahead]),
                (do_hbm.at[:, ahead], do_ref.at[:, ahead]),
                (k_hbm, k_ref),
                (v_hbm, v_ref),
                (q_hbm.at[:, rest], q_ref.at[:, rest]),
                (do_hbm.at[:, rest], do_ref.at[:, rest]),
                (o_hbm, o_ref),
                (lse_hbm, lse_ref),
            )
        )
    ]
    for load in loads:
        load.start()

    barrier = pltpu.get_barrier_semaphore()
    for other in (right, left, below, above):
        pl.semaphore_signal(barrier, inc=1, device_id=other, device_id_type=MESH)

    @pl.when(leaps)
    def _():
        pl.semaphore_signal(barrier, inc=1, device_id=leap_to, device_id_type=MESH)

    @pl.when(lands)
    def _():
        pl.semaphore_signal(barrier, inc=1, device_id=leap_from, device_id_type=MESH)

    @pl.when(leaps | lands)
    def _():
        pl.semaphore_wait(barrier, 5)

    @pl.when(jnp.logical_not(leaps | lands))
    def _():
        pl.semaphore_wait(barrier, 4)

    def message(kind, g):
        if kind in (Q1, Q2, Q3):
            src, dst, to = visit.at[kind, g], visit.at[kind + 1, g], right
        elif kind == KV:
            src = kvb.at[g, :, pl.ds(0, BLOCK), :]
            dst = kvb.at[g, :, pl.ds(BLOCK, BLOCK), :]
            to = above
        elif kind == GKV:
            src, dst, to = gkv_send.at[g], gkv_recv.at[g], below
        else:
            src, dst, to = gq_send.at[kind - R3, g], gq_recv.at[kind - R3, g], left
        return pltpu.make_async_remote_copy(
            src_ref=src, dst_ref=dst,
            send_sem=send_sem.at[kind, g], recv_sem=recv_sem.at[kind, g],
            device_id=to, device_id_type=MESH,
        )

    def leap_query(g):
        return pltpu.make_async_remote_copy(
            src_ref=visit.at[0, g], dst_ref=visit.at[WINDOW - 1, g],
            send_sem=leap_send.at[g], recv_sem=recv_sem.at[Q3, g],
            device_id=leap_to, device_id_type=MESH,
        )

    def leap_gradient(g):
        return pltpu.make_async_remote_copy(
            src_ref=gq_send.at[0, g], dst_ref=gq_leap.at[g],
            send_sem=send_sem.at[R3, g], recv_sem=leap_recv.at[g],
            device_id=leap_from, device_id_type=MESH,
        )

    def stat_message(w):
        return pltpu.make_async_remote_copy(
            src_ref=stats.at[w], dst_ref=stats.at[w + 1],
            send_sem=stat_send.at[w], recv_sem=stat_recv.at[w],
            device_id=right, device_id_type=MESH,
        )

    def columns(g):
        return pl.ds(pl.multiple_of(g * width, width), width)

    def begin_queries(g):
        here = columns(g)
        visit[0, g, 0] = q_ref[:, here]
        visit[0, g, 1] = do_ref[:, here]
        message(Q1, g).start()

        @pl.when(leaps)
        def _():
            leap_query(g).start()

    def begin_keys(g):
        here = columns(g)
        kvb[g, 0, pl.ds(0, BLOCK), :] = k_ref[:, here]
        kvb[g, 1, pl.ds(0, BLOCK), :] = v_ref[:, here]
        message(KV, g).start()

    def make_stats():
        ones = jnp.ones((8, HEAD_DIM), jnp.bfloat16)
        stats[0, pl.ds(0, heads), :] = lse_ref[...]
        for h in range(heads):
            part = pl.ds(h * HEAD_DIM, HEAD_DIM)
            product = do_ref[:, part].astype(jnp.float32) * o_ref[:, part].astype(jnp.float32)
            high = product.astype(jnp.bfloat16)
            low = (product - high.astype(jnp.float32)).astype(jnp.bfloat16)
            delta = dot(ones, high, 1, 1) + dot(ones, low, 1, 1)
            stats[0, pl.ds(heads + h, 1), :] = delta[0:1]
        for a in range(2):
            for w in range(WINDOW):
                blocked = (1 - adj_ref[0, a, 0, w]).astype(jnp.float32) * BIG
                stats[0, pl.ds(2 * heads + a * WINDOW + w, 1), :] = jnp.full((1, BLOCK), blocked, jnp.float32)

    def pair_terms(g, first):
        pair = (first, first + 1)
        span = pl.ds(first * BLOCK, 2 * BLOCK)
        kk = kvb[g, 0]
        vv = kvb[g, 1]
        qq = visit[first : first + 2, g, 0].reshape(2 * BLOCK, HEAD_DIM)
        dd = visit[first : first + 2, g, 1].reshape(2 * BLOCK, HEAD_DIM)
        delta = jnp.concatenate([stats[w, pl.ds(heads + g, 1), :] for w in pair], axis=1)
        for a in range(2):
            norms = jnp.concatenate(
                [
                    stats[w, pl.ds(g, 1), :] + stats[w, pl.ds(2 * heads + a * WINDOW + w, 1), :]
                    for w in pair
                ],
                axis=1,
            )
            half = slice(a * BLOCK, (a + 1) * BLOCK)
            prob = jnp.exp(dot(kk[half], qq, 1, 1) * inverse - norms)
            probs[g, half, span] = prob.astype(jnp.bfloat16)
            prob_grad = dot(vv[half], dd, 1, 1)
            score_grad = prob * (prob_grad - delta) * inverse
            score_grads[g, half, span] = score_grad.astype(jnp.bfloat16)
        return dot(score_grads[g, :, span], kk, 0, 0)

    def work_near(g):
        message(KV, g).wait_recv()
        grad_q = pair_terms(g, 0)
        gq_part[0, g] = grad_q[:BLOCK]
        gq_part[1, g] = grad_q[BLOCK:]

    def work_far(g):
        message(Q3, g).wait_recv()
        grad_q = pair_terms(g, 2)
        gq_part[2, g] = grad_q[:BLOCK]
        gq_send[0, g] = grad_q[BLOCK:].astype(jnp.bfloat16)

        @pl.when(lands)
        def _():
            leap_gradient(g).start()

        @pl.when(jnp.logical_not(lands))
        def _():
            message(R3, g).start()

        qq = visit[:, g, 0].reshape(WINDOW * BLOCK, HEAD_DIM)
        dd = visit[:, g, 1].reshape(WINDOW * BLOCK, HEAD_DIM)
        for n, total in ((0, dot(score_grads[g], qq, 1, 0)), (1, dot(probs[g], dd, 1, 0))):
            gkv_near[g, n] = total[:BLOCK]
            gkv_send[g, n] = total[BLOCK:].astype(jnp.bfloat16)
        message(GKV, g).start()

    def add_second(g):
        @pl.when(skips)
        def _():
            gq_send[1, g] = gq_part[2, g].astype(jnp.bfloat16)

        @pl.when(jnp.logical_not(skips))
        def _():
            message(R3, g).wait_recv()
            total = gq_recv[0, g].astype(jnp.float32) + gq_part[2, g]
            gq_send[1, g] = total.astype(jnp.bfloat16)

        message(R2, g).start()

    def add_first(g):
        message(R2, g).wait_recv()
        total = gq_recv[1, g].astype(jnp.float32) + gq_part[1, g]
        gq_send[2, g] = total.astype(jnp.bfloat16)
        message(R1, g).start()

    def store(n, g):
        out = (gq_out, gk_out, gv_out)[n]
        return pltpu.make_async_copy(done.at[n, g], out.at[:, columns(g)], done_sem.at[n, g])

    def finish(g):
        message(R1, g).wait_recv()
        total = gq_recv[2, g].astype(jnp.float32) + gq_part[0, g]

        @pl.when(leaps)
        def _():
            leap_gradient(g).wait_recv()
            done[0, g] = (total + gq_leap[g].astype(jnp.float32)).astype(jnp.bfloat16)

        @pl.when(jnp.logical_not(leaps))
        def _():
            done[0, g] = total.astype(jnp.bfloat16)

        message(GKV, g).wait_recv()
        for n in range(2):
            total = gkv_near[g, n] + gkv_recv[g, n].astype(jnp.float32)
            done[n + 1, g] = total.astype(jnp.bfloat16)
        for n in range(3):
            store(n, g).start()
        for kind in range(KINDS):
            if kind != Q3:
                message(kind, g).wait_send()

        @pl.when(jnp.logical_not(skips))
        def _():
            message(Q3, g).wait_send()

        @pl.when(leaps)
        def _():
            leap_query(g).wait_send()

    def settle(g):
        for n in range(3):
            store(n, g).wait()

    def at(i, skew, action):
        g = i - skew

        @pl.when((g >= 0) & (g < groups))
        def _():
            action(g)

    def forward_first(g):
        message(Q1, g).wait_recv()
        message(Q2, g).start()

    def forward_second(g):
        message(Q2, g).wait_recv()

        @pl.when(jnp.logical_not(skips))
        def _():
            message(Q3, g).start()

    def stats_forward(w):
        stat_message(w - 1).wait_recv()
        stat_message(w).start()

    def turn(i, carry):
        at(i, -AHEAD, begin_queries)
        at(i, -AHEAD, begin_keys)
        at(i, 0, forward_first)

        @pl.when(i == 0)
        def _():
            stats_forward(1)

        at(i, 1, work_near)
        at(i, 2, forward_second)

        @pl.when(i == 2)
        def _():
            stats_forward(2)

        @pl.when(i == 4)
        def _():
            stat_message(2).wait_recv()

        at(i, 4, work_far)
        at(i, 6, add_second)
        at(i, 8, add_first)
        at(i, 10, finish)
        at(i, 12, settle)
        return carry

    for load in loads[:2]:
        load.wait()
    for g in range(AHEAD):
        begin_queries(g)
    for load in loads[2:4]:
        load.wait()
    for g in range(AHEAD):
        begin_keys(g)
    for load in loads[4:]:
        load.wait()
    make_stats()
    stat_message(0).start()

    lax.fori_loop(0, groups + 12, turn, 0)

    for w in range(WINDOW - 1):
        stat_message(w).wait_send()


def store_kernel(a_ref, b_ref, c_ref, a_out, b_out, c_out, held, in_sem, out_sem):
    half = a_ref.shape[0] // 2
    refs = ((a_ref, a_out), (b_ref, b_out), (c_ref, c_out))
    pieces = [(n, p, pl.ds(p * half, half)) for p in range(2) for n in range(3)]
    fetches = [
        pltpu.make_async_copy(refs[n][0].at[here], held.at[n, here], in_sem.at[n, p])
        for n, p, here in pieces
    ]
    stores = [
        pltpu.make_async_copy(held.at[n, here], refs[n][1].at[here], out_sem.at[n, p])
        for n, p, here in pieces
    ]
    for fetch in fetches:
        fetch.start()
    for fetch, store in zip(fetches, stores):
        fetch.wait()
        store.start()
    for store in stores:
        store.wait()


def local(rows, cols, queries, keys, values, outputs, d_out, row_lse, adjacency):
    tokens, features = queries.shape
    heads = features // HEAD_DIM
    groups = heads
    width = HEAD_DIM
    low, wide = jnp.bfloat16, jnp.float32
    hbm = pl.BlockSpec(memory_space=pltpu.HBM)
    out = jax.ShapeDtypeStruct((tokens, features), low)
    pairs = 2 * WINDOW * heads
    grads = pl.pallas_call(
        functools.partial(kernel, rows, cols, groups, heads),
        out_shape=(out, out, out),
        in_specs=[hbm] * 6 + [pl.BlockSpec(memory_space=pltpu.SMEM)],
        out_specs=(hbm, hbm, hbm),
        scratch_shapes=[pltpu.VMEM((tokens, features), low)] * 5
        + [
            pltpu.VMEM((heads, tokens), wide),
            pltpu.SemaphoreType.DMA((8,)),
            pltpu.VMEM((3, groups, BLOCK, width), low),
            pltpu.SemaphoreType.DMA((3, groups)),
            pltpu.VMEM((WINDOW, groups, 2, BLOCK, width), low),
            pltpu.VMEM((groups, 2, 2 * BLOCK, width), low),
            pltpu.VMEM((WINDOW, 2 * heads + 2 * WINDOW, BLOCK), wide),
            pltpu.VMEM((groups, 2 * BLOCK, WINDOW * BLOCK), low),
            pltpu.VMEM((groups, 2 * BLOCK, WINDOW * BLOCK), low),
            pltpu.VMEM((WINDOW - 1, groups, BLOCK, width), wide),
            pltpu.VMEM((groups, 2, BLOCK, width), wide),
            pltpu.VMEM((WINDOW - 1, groups, BLOCK, width), low),
            pltpu.VMEM((WINDOW - 1, groups, BLOCK, width), low),
            pltpu.VMEM((groups, 2, BLOCK, width), low),
            pltpu.VMEM((groups, 2, BLOCK, width), low),
            pltpu.SemaphoreType.DMA((KINDS, groups)),
            pltpu.SemaphoreType.DMA((KINDS, groups)),
            pltpu.SemaphoreType.DMA((WINDOW - 1,)),
            pltpu.SemaphoreType.DMA((WINDOW - 1,)),
            pltpu.VMEM((groups, BLOCK, width), low),
            pltpu.SemaphoreType.DMA((groups,)),
            pltpu.SemaphoreType.DMA((groups,)),
        ],
        compiler_params=pltpu.CompilerParams(
            collective_id=0, has_side_effects=True, vmem_limit_bytes=62 * 1024 * 1024
        ),
        cost_estimate=pl.CostEstimate(
            flops=pairs * 5 * 2 * BLOCK * BLOCK * HEAD_DIM,
            bytes_accessed=8 * tokens * features * 2,
            transcendentals=pairs * BLOCK * BLOCK,
        ),
        name="block_sparse_backward",
    )(queries, keys, values, outputs, d_out, row_lse, adjacency.transpose(0, 1, 3, 2))
    return pl.pallas_call(
        store_kernel,
        out_shape=(out, out, out),
        in_specs=[hbm] * 3,
        out_specs=(hbm, hbm, hbm),
        scratch_shapes=[
            pltpu.VMEM((3, tokens, features), low),
            pltpu.SemaphoreType.DMA((3, 2)),
            pltpu.SemaphoreType.DMA((3, 2)),
        ],
        compiler_params=pltpu.CompilerParams(vmem_limit_bytes=62 * 1024 * 1024),
        name="store_gradients",
    )(*grads)


def solution(mesh):
    token_rows = P(("pb", "ka"), None)
    placed = (token_rows,) * 5 + (P(None, ("pb", "ka")), P(("pb", "ka"), None, None, None))
    return jax.shard_map(
        functools.partial(local, mesh.shape["pb"], mesh.shape["ka"]),
        mesh=mesh,
        in_specs=placed,
        out_specs=(token_rows, token_rows, token_rows),
        check_vma=False,
    )
```

```python
import functools
import math

import jax
import jax.numpy as jnp
from jax import lax
from jax.experimental import pallas as pl
from jax.experimental.pallas import tpu as pltpu
from jax.sharding import PartitionSpec as P

HEAD_DIM = 128
BLOCK = 128
WINDOW = 4
AHEAD = 8
BIG = 1e30
MESH = pl.DeviceIdType.MESH

Q1, Q2, Q3, KV, R3, R2, R1, GKV = range(8)
KINDS = 8


def dot(a, b, da, db):
    return lax.dot_general(a, b, (((da,), (db,)), ((), ())), preferred_element_type=jnp.float32)


def kernel(
    rows, cols, groups, heads,
    q_hbm, k_hbm, v_hbm, o_hbm, do_hbm, lse_hbm, adj_ref,
    gq_out, gk_out, gv_out,
    q_ref, k_ref, v_ref, o_ref, do_ref, lse_ref, load_sem, done, done_sem,
    visit, kvb, stats, probs, score_grads, gq_part, gkv_near, gq_send, gq_recv, gkv_send, gkv_recv,
    send_sem, recv_sem, stat_send, stat_recv, gq_leap, leap_send, leap_recv,
):
    inverse = 1.0 / math.sqrt(HEAD_DIM)
    width = HEAD_DIM
    r = lax.axis_index("pb")
    c = lax.axis_index("ka")
    right = (r, lax.rem(c + 1, cols))
    left = (r, lax.rem(c + cols - 1, cols))
    below = (lax.rem(r + 1, rows), c)
    above = (lax.rem(r + rows - 1, rows), c)
    leaps = c == cols - (WINDOW - 1)
    lands = c == 0
    skips = c == cols - 1
    leap_to = (r, 0)
    leap_from = (r, cols - (WINDOW - 1))

    ahead = pl.ds(0, AHEAD * width)
    rest = pl.ds(AHEAD * width, (groups - AHEAD) * width)
    loads = [
        pltpu.make_async_copy(source, target, load_sem.at[n])
        for n, (source, target) in enumerate(
            (
                (q_hbm.at[:, ahead], q_ref.at[:, ahead]),
                (do_hbm.at[:, ahead], do_ref.at[:, ahead]),
                (k_hbm, k_ref),
                (v_hbm, v_ref),
                (q_hbm.at[:, rest], q_ref.at[:, rest]),
                (do_hbm.at[:, rest], do_ref.at[:, rest]),
                (o_hbm, o_ref),
                (lse_hbm, lse_ref),
            )
        )
    ]
    for load in loads:
        load.start()

    barrier = pltpu.get_barrier_semaphore()
    for other in (right, left, below, above):
        pl.semaphore_signal(barrier, inc=1, device_id=other, device_id_type=MESH)

    @pl.when(leaps)
    def _():
        pl.semaphore_signal(barrier, inc=1, device_id=leap_to, device_id_type=MESH)

    @pl.when(lands)
    def _():
        pl.semaphore_signal(barrier, inc=1, device_id=leap_from, device_id_type=MESH)

    @pl.when(leaps | lands)
    def _():
        pl.semaphore_wait(barrier, 5)

    @pl.when(jnp.logical_not(leaps | lands))
    def _():
        pl.semaphore_wait(barrier, 4)

    def message(kind, g):
        if kind in (Q1, Q2, Q3):
            src, dst, to = visit.at[kind, g], visit.at[kind + 1, g], right
        elif kind == KV:
            src = kvb.at[g, :, pl.ds(0, BLOCK), :]
            dst = kvb.at[g, :, pl.ds(BLOCK, BLOCK), :]
            to = above
        elif kind == GKV:
            src, dst, to = gkv_send.at[g], gkv_recv.at[g], below
        else:
            src, dst, to = gq_send.at[kind - R3, g], gq_recv.at[kind - R3, g], left
        return pltpu.make_async_remote_copy(
            src_ref=src, dst_ref=dst,
            send_sem=send_sem.at[kind, g], recv_sem=recv_sem.at[kind, g],
            device_id=to, device_id_type=MESH,
        )

    def leap_query(g):
        return pltpu.make_async_remote_copy(
            src_ref=visit.at[0, g], dst_ref=visit.at[WINDOW - 1, g],
            send_sem=leap_send.at[g], recv_sem=recv_sem.at[Q3, g],
            device_id=leap_to, device_id_type=MESH,
        )

    def leap_gradient(g):
        return pltpu.make_async_remote_copy(
            src_ref=gq_send.at[0, g], dst_ref=gq_leap.at[g],
            send_sem=send_sem.at[R3, g], recv_sem=leap_recv.at[g],
            device_id=leap_from, device_id_type=MESH,
        )

    def stat_message(w):
        return pltpu.make_async_remote_copy(
            src_ref=stats.at[w], dst_ref=stats.at[w + 1],
            send_sem=stat_send.at[w], recv_sem=stat_recv.at[w],
            device_id=right, device_id_type=MESH,
        )

    def columns(g):
        return pl.ds(pl.multiple_of(g * width, width), width)

    def begin_queries(g):
        here = columns(g)
        visit[0, g, 0] = q_ref[:, here]
        visit[0, g, 1] = do_ref[:, here]
        message(Q1, g).start()

        @pl.when(leaps)
        def _():
            leap_query(g).start()

    def begin_keys(g):
        here = columns(g)
        kvb[g, 0, pl.ds(0, BLOCK), :] = k_ref[:, here]
        kvb[g, 1, pl.ds(0, BLOCK), :] = v_ref[:, here]
        message(KV, g).start()

    def make_stats():
        ones = jnp.ones((8, HEAD_DIM), jnp.bfloat16)
        stats[0, pl.ds(0, heads), :] = lse_ref[...]
        for h in range(heads):
            part = pl.ds(h * HEAD_DIM, HEAD_DIM)
            product = do_ref[:, part].astype(jnp.float32) * o_ref[:, part].astype(jnp.float32)
            high = product.astype(jnp.bfloat16)
            low = (product - high.astype(jnp.float32)).astype(jnp.bfloat16)
            delta = dot(ones, high, 1, 1) + dot(ones, low, 1, 1)
            stats[0, pl.ds(heads + h, 1), :] = delta[0:1]
        for a in range(2):
            for w in range(WINDOW):
                blocked = (1 - adj_ref[0, a, 0, w]).astype(jnp.float32) * BIG
                stats[0, pl.ds(2 * heads + a * WINDOW + w, 1), :] = jnp.full((1, BLOCK), blocked, jnp.float32)

    def pair_terms(g, first):
        pair = (first, first + 1)
        span = pl.ds(first * BLOCK, 2 * BLOCK)
        kk = kvb[g, 0]
        vv = kvb[g, 1]
        qq = visit[first : first + 2, g, 0].reshape(2 * BLOCK, HEAD_DIM)
        dd = visit[first : first + 2, g, 1].reshape(2 * BLOCK, HEAD_DIM)
        delta = jnp.concatenate([stats[w, pl.ds(heads + g, 1), :] for w in pair], axis=1)
        for a in range(2):
            norms = jnp.concatenate(
                [
                    stats[w, pl.ds(g, 1), :] + stats[w, pl.ds(2 * heads + a * WINDOW + w, 1), :]
                    for w in pair
                ],
                axis=1,
            )
            half = slice(a * BLOCK, (a + 1) * BLOCK)
            prob = jnp.exp(dot(kk[half], qq, 1, 1) * inverse - norms)
            probs[g, half, span] = prob.astype(jnp.bfloat16)
            prob_grad = dot(vv[half], dd, 1, 1)
            score_grad = prob * (prob_grad - delta) * inverse
            score_grads[g, half, span] = score_grad.astype(jnp.bfloat16)
        return dot(score_grads[g, :, span], kk, 0, 0)

    def work_near(g):
        message(KV, g).wait_recv()
        grad_q = pair_terms(g, 0)
        gq_part[0, g] = grad_q[:BLOCK]
        gq_part[1, g] = grad_q[BLOCK:]

    def work_far(g):
        message(Q3, g).wait_recv()
        grad_q = pair_terms(g, 2)
        gq_part[2, g] = grad_q[:BLOCK]
        gq_send[0, g] = grad_q[BLOCK:].astype(jnp.bfloat16)

        @pl.when(lands)
        def _():
            leap_gradient(g).start()

        @pl.when(jnp.logical_not(lands))
        def _():
            message(R3, g).start()

        qq = visit[:, g, 0].reshape(WINDOW * BLOCK, HEAD_DIM)
        dd = visit[:, g, 1].reshape(WINDOW * BLOCK, HEAD_DIM)
        for n, total in ((0, dot(score_grads[g], qq, 1, 0)), (1, dot(probs[g], dd, 1, 0))):
            gkv_near[g, n] = total[:BLOCK]
            gkv_send[g, n] = total[BLOCK:].astype(jnp.bfloat16)
        message(GKV, g).start()

    def add_second(g):
        @pl.when(skips)
        def _():
            gq_send[1, g] = gq_part[2, g].astype(jnp.bfloat16)

        @pl.when(jnp.logical_not(skips))
        def _():
            message(R3, g).wait_recv()
            total = gq_recv[0, g].astype(jnp.float32) + gq_part[2, g]
            gq_send[1, g] = total.astype(jnp.bfloat16)

        message(R2, g).start()

    def add_first(g):
        message(R2, g).wait_recv()
        total = gq_recv[1, g].astype(jnp.float32) + gq_part[1, g]
        gq_send[2, g] = total.astype(jnp.bfloat16)
        message(R1, g).start()

    def store(n, g):
        out = (gq_out, gk_out, gv_out)[n]
        return pltpu.make_async_copy(done.at[n, g], out.at[:, columns(g)], done_sem.at[n, g])

    def finish(g):
        message(R1, g).wait_recv()
        total = gq_recv[2, g].astype(jnp.float32) + gq_part[0, g]

        @pl.when(leaps)
        def _():
            leap_gradient(g).wait_recv()
            done[0, g] = (total + gq_leap[g].astype(jnp.float32)).astype(jnp.bfloat16)

        @pl.when(jnp.logical_not(leaps))
        def _():
            done[0, g] = total.astype(jnp.bfloat16)

        message(GKV, g).wait_recv()
        for n in range(2):
            total = gkv_near[g, n] + gkv_recv[g, n].astype(jnp.float32)
            done[n + 1, g] = total.astype(jnp.bfloat16)
        for n in range(3):
            store(n, g).start()
        for kind in range(KINDS):
            if kind != Q3:
                message(kind, g).wait_send()

        @pl.when(jnp.logical_not(skips))
        def _():
            message(Q3, g).wait_send()

        @pl.when(leaps)
        def _():
            leap_query(g).wait_send()

    def settle(g):
        for n in range(3):
            store(n, g).wait()

    def at(i, skew, action):
        g = i - skew

        @pl.when((g >= 0) & (g < groups))
        def _():
            action(g)

    def forward_first(g):
        message(Q1, g).wait_recv()
        message(Q2, g).start()

    def forward_second(g):
        message(Q2, g).wait_recv()

        @pl.when(jnp.logical_not(skips))
        def _():
            message(Q3, g).start()

    def stats_forward(w):
        stat_message(w - 1).wait_recv()
        stat_message(w).start()

    def turn(i, carry):
        at(i, -AHEAD, begin_queries)
        at(i, 0, forward_first)

        @pl.when(i == 0)
        def _():
            stats_forward(1)

        at(i, 1, work_near)
        at(i, 2, forward_second)

        @pl.when(i == 2)
        def _():
            stats_forward(2)

        @pl.when(i == 4)
        def _():
            stat_message(2).wait_recv()

        at(i, 4, work_far)
        at(i, 6, add_second)
        at(i, 8, add_first)
        at(i, 10, finish)
        at(i, 12, settle)
        return carry

    for load in loads[:2]:
        load.wait()

    def begin_some_queries(g, carry):
        begin_queries(g)
        return carry

    lax.fori_loop(0, AHEAD, begin_some_queries, 0)
    for load in loads[2:4]:
        load.wait()

    def begin_all_keys(g, carry):
        begin_keys(g)
        return carry

    lax.fori_loop(0, groups, begin_all_keys, 0)
    for load in loads[4:]:
        load.wait()
    make_stats()
    stat_message(0).start()

    lax.fori_loop(0, groups + 12, turn, 0)

    for w in range(WINDOW - 1):
        stat_message(w).wait_send()


def store_kernel(a_ref, b_ref, c_ref, a_out, b_out, c_out, held, in_sem, out_sem):
    half = a_ref.shape[0] // 2
    refs = ((a_ref, a_out), (b_ref, b_out), (c_ref, c_out))
    pieces = [(n, p, pl.ds(p * half, half)) for p in range(2) for n in range(3)]
    fetches = [
        pltpu.make_async_copy(refs[n][0].at[here], held.at[n, here], in_sem.at[n, p])
        for n, p, here in pieces
    ]
    stores = [
        pltpu.make_async_copy(held.at[n, here], refs[n][1].at[here], out_sem.at[n, p])
        for n, p, here in pieces
    ]
    for fetch in fetches:
        fetch.start()
    for fetch, store in zip(fetches, stores):
        fetch.wait()
        store.start()
    for store in stores:
        store.wait()


def local(rows, cols, queries, keys, values, outputs, d_out, row_lse, adjacency):
    tokens, features = queries.shape
    heads = features // HEAD_DIM
    groups = heads
    width = HEAD_DIM
    low, wide = jnp.bfloat16, jnp.float32
    hbm = pl.BlockSpec(memory_space=pltpu.HBM)
    out = jax.ShapeDtypeStruct((tokens, features), low)
    pairs = 2 * WINDOW * heads
    grads = pl.pallas_call(
        functools.partial(kernel, rows, cols, groups, heads),
        out_shape=(out, out, out),
        in_specs=[hbm] * 6 + [pl.BlockSpec(memory_space=pltpu.SMEM)],
        out_specs=(hbm, hbm, hbm),
        scratch_shapes=[pltpu.VMEM((tokens, features), low)] * 5
        + [
            pltpu.VMEM((heads, tokens), wide),
            pltpu.SemaphoreType.DMA((8,)),
            pltpu.VMEM((3, groups, BLOCK, width), low),
            pltpu.SemaphoreType.DMA((3, groups)),
            pltpu.VMEM((WINDOW, groups, 2, BLOCK, width), low),
            pltpu.VMEM((groups, 2, 2 * BLOCK, width), low),
            pltpu.VMEM((WINDOW, 2 * heads + 2 * WINDOW, BLOCK), wide),
            pltpu.VMEM((groups, 2 * BLOCK, WINDOW * BLOCK), low),
            pltpu.VMEM((groups, 2 * BLOCK, WINDOW * BLOCK), low),
            pltpu.VMEM((WINDOW - 1, groups, BLOCK, width), wide),
            pltpu.VMEM((groups, 2, BLOCK, width), wide),
            pltpu.VMEM((WINDOW - 1, groups, BLOCK, width), low),
            pltpu.VMEM((WINDOW - 1, groups, BLOCK, width), low),
            pltpu.VMEM((groups, 2, BLOCK, width), low),
            pltpu.VMEM((groups, 2, BLOCK, width), low),
            pltpu.SemaphoreType.DMA((KINDS, groups)),
            pltpu.SemaphoreType.DMA((KINDS, groups)),
            pltpu.SemaphoreType.DMA((WINDOW - 1,)),
            pltpu.SemaphoreType.DMA((WINDOW - 1,)),
            pltpu.VMEM((groups, BLOCK, width), low),
            pltpu.SemaphoreType.DMA((groups,)),
            pltpu.SemaphoreType.DMA((groups,)),
        ],
        compiler_params=pltpu.CompilerParams(
            collective_id=0, has_side_effects=True, vmem_limit_bytes=62 * 1024 * 1024
        ),
        cost_estimate=pl.CostEstimate(
            flops=pairs * 5 * 2 * BLOCK * BLOCK * HEAD_DIM,
            bytes_accessed=8 * tokens * features * 2,
            transcendentals=pairs * BLOCK * BLOCK,
        ),
        name="block_sparse_backward",
    )(queries, keys, values, outputs, d_out, row_lse, adjacency.transpose(0, 1, 3, 2))
    return pl.pallas_call(
        store_kernel,
        out_shape=(out, out, out),
        in_specs=[hbm] * 3,
        out_specs=(hbm, hbm, hbm),
        scratch_shapes=[
            pltpu.VMEM((3, tokens, features), low),
            pltpu.SemaphoreType.DMA((3, 2)),
            pltpu.SemaphoreType.DMA((3, 2)),
        ],
        compiler_params=pltpu.CompilerParams(vmem_limit_bytes=62 * 1024 * 1024),
        name="store_gradients",
    )(*grads)


def solution(mesh):
    token_rows = P(("pb", "ka"), None)
    placed = (token_rows,) * 5 + (P(None, ("pb", "ka")), P(("pb", "ka"), None, None, None))
    return jax.shard_map(
        functools.partial(local, mesh.shape["pb"], mesh.shape["ka"]),
        mesh=mesh,
        in_specs=placed,
        out_specs=(token_rows, token_rows, token_rows),
        check_vma=False,
    )
```

```python
import functools
import math

import jax
import jax.numpy as jnp
from jax import lax
from jax.experimental import pallas as pl
from jax.experimental.pallas import tpu as pltpu
from jax.sharding import PartitionSpec as P

HEAD_DIM = 128
BLOCK = 128
WINDOW = 4
AHEAD = 4
GROUP_HEADS = 2
BIG = 1e30
MESH = pl.DeviceIdType.MESH

Q1, Q2, Q3, KV, R3, R2, R1, GKV = range(8)
KINDS = 8


def dot(a, b, da, db):
    return lax.dot_general(a, b, (((da,), (db,)), ((), ())), preferred_element_type=jnp.float32)


def kernel(
    rows, cols, groups, heads,
    q_hbm, k_hbm, v_hbm, o_hbm, do_hbm, lse_hbm, adj_ref,
    gq_out, gk_out, gv_out,
    q_ref, k_ref, v_ref, o_ref, do_ref, lse_ref, load_sem, done, done_sem,
    visit, kvb, stats, probs, score_grads, gq_part, gkv_near, gq_send, gq_recv, gkv_send, gkv_recv,
    send_sem, recv_sem, stat_send, stat_recv, gq_leap, leap_send, leap_recv,
):
    inverse = 1.0 / math.sqrt(HEAD_DIM)
    width = GROUP_HEADS * HEAD_DIM
    r = lax.axis_index("pb")
    c = lax.axis_index("ka")
    right = (r, lax.rem(c + 1, cols))
    left = (r, lax.rem(c + cols - 1, cols))
    below = (lax.rem(r + 1, rows), c)
    above = (lax.rem(r + rows - 1, rows), c)
    leaps = c == cols - (WINDOW - 1)
    lands = c == 0
    skips = c == cols - 1
    leap_to = (r, 0)
    leap_from = (r, cols - (WINDOW - 1))

    ahead = pl.ds(0, AHEAD * width)
    rest = pl.ds(AHEAD * width, (groups - AHEAD) * width)
    loads = [
        pltpu.make_async_copy(source, target, load_sem.at[n])
        for n, (source, target) in enumerate(
            (
                (q_hbm.at[:, ahead], q_ref.at[:, ahead]),
                (do_hbm.at[:, ahead], do_ref.at[:, ahead]),
                (k_hbm, k_ref),
                (v_hbm, v_ref),
                (q_hbm.at[:, rest], q_ref.at[:, rest]),
                (do_hbm.at[:, rest], do_ref.at[:, rest]),
                (o_hbm, o_ref),
                (lse_hbm, lse_ref),
            )
        )
    ]
    for load in loads:
        load.start()

    barrier = pltpu.get_barrier_semaphore()
    for other in (right, left, below, above):
        pl.semaphore_signal(barrier, inc=1, device_id=other, device_id_type=MESH)

    @pl.when(leaps)
    def _():
        pl.semaphore_signal(barrier, inc=1, device_id=leap_to, device_id_type=MESH)

    @pl.when(lands)
    def _():
        pl.semaphore_signal(barrier, inc=1, device_id=leap_from, device_id_type=MESH)

    @pl.when(leaps | lands)
    def _():
        pl.semaphore_wait(barrier, 5)

    @pl.when(jnp.logical_not(leaps | lands))
    def _():
        pl.semaphore_wait(barrier, 4)

    def message(kind, g):
        if kind in (Q1, Q2, Q3):
            src, dst, to = visit.at[kind, g], visit.at[kind + 1, g], right
        elif kind == KV:
            src = kvb.at[g, :, pl.ds(0, BLOCK), :]
            dst = kvb.at[g, :, pl.ds(BLOCK, BLOCK), :]
            to = above
        elif kind == GKV:
            src, dst, to = gkv_send.at[g], gkv_recv.at[g], below
        else:
            src, dst, to = gq_send.at[kind - R3, g], gq_recv.at[kind - R3, g], left
        return pltpu.make_async_remote_copy(
            src_ref=src, dst_ref=dst,
            send_sem=send_sem.at[kind, g], recv_sem=recv_sem.at[kind, g],
            device_id=to, device_id_type=MESH,
        )

    def leap_query(g):
        return pltpu.make_async_remote_copy(
            src_ref=visit.at[0, g], dst_ref=visit.at[WINDOW - 1, g],
            send_sem=leap_send.at[g], recv_sem=recv_sem.at[Q3, g],
            device_id=leap_to, device_id_type=MESH,
        )

    def leap_gradient(g):
        return pltpu.make_async_remote_copy(
            src_ref=gq_send.at[0, g], dst_ref=gq_leap.at[g],
            send_sem=send_sem.at[R3, g], recv_sem=leap_recv.at[g],
            device_id=leap_from, device_id_type=MESH,
        )

    def stat_message(w):
        return pltpu.make_async_remote_copy(
            src_ref=stats.at[w], dst_ref=stats.at[w + 1],
            send_sem=stat_send.at[w], recv_sem=stat_recv.at[w],
            device_id=right, device_id_type=MESH,
        )

    def columns(g):
        return pl.ds(pl.multiple_of(g * width, width), width)

    def begin_queries(g):
        here = columns(g)
        visit[0, g, 0] = q_ref[:, here]
        visit[0, g, 1] = do_ref[:, here]
        message(Q1, g).start()

        @pl.when(leaps)
        def _():
            leap_query(g).start()

    def begin_keys(g):
        here = columns(g)
        kvb[g, 0, pl.ds(0, BLOCK), :] = k_ref[:, here]
        kvb[g, 1, pl.ds(0, BLOCK), :] = v_ref[:, here]
        message(KV, g).start()

    def make_stats():
        ones = jnp.ones((8, HEAD_DIM), jnp.bfloat16)
        stats[0, pl.ds(0, heads), :] = lse_ref[...]
        for h in range(heads):
            part = pl.ds(h * HEAD_DIM, HEAD_DIM)
            product = do_ref[:, part].astype(jnp.float32) * o_ref[:, part].astype(jnp.float32)
            high = product.astype(jnp.bfloat16)
            low = (product - high.astype(jnp.float32)).astype(jnp.bfloat16)
            delta = dot(ones, high, 1, 1) + dot(ones, low, 1, 1)
            stats[0, pl.ds(heads + h, 1), :] = delta[0:1]
        for a in range(2):
            for w in range(WINDOW):
                blocked = (1 - adj_ref[0, a, 0, w]).astype(jnp.float32) * BIG
                stats[0, pl.ds(2 * heads + a * WINDOW + w, 1), :] = jnp.full((1, BLOCK), blocked, jnp.float32)

    def part(hh):
        return slice(hh * HEAD_DIM, (hh + 1) * HEAD_DIM)

    def pair_terms(g, hh, first):
        h = g * GROUP_HEADS + hh
        pair = (first, first + 1)
        span = pl.ds(first * BLOCK, 2 * BLOCK)
        kk = kvb[g, 0, :, part(hh)]
        vv = kvb[g, 1, :, part(hh)]
        qq = visit[first : first + 2, g, 0, :, part(hh)].reshape(2 * BLOCK, HEAD_DIM)
        dd = visit[first : first + 2, g, 1, :, part(hh)].reshape(2 * BLOCK, HEAD_DIM)
        delta = jnp.concatenate([stats[w, pl.ds(heads + h, 1), :] for w in pair], axis=1)
        for a in range(2):
            norms = jnp.concatenate(
                [
                    stats[w, pl.ds(h, 1), :] + stats[w, pl.ds(2 * heads + a * WINDOW + w, 1), :]
                    for w in pair
                ],
                axis=1,
            )
            half = slice(a * BLOCK, (a + 1) * BLOCK)
            prob = jnp.exp(dot(kk[half], qq, 1, 1) * inverse - norms)
            probs[h, half, span] = prob.astype(jnp.bfloat16)
            prob_grad = dot(vv[half], dd, 1, 1)
            score_grad = prob * (prob_grad - delta) * inverse
            score_grads[h, half, span] = score_grad.astype(jnp.bfloat16)
        return dot(score_grads[h, :, span], kk, 0, 0)

    def work_near(g):
        message(KV, g).wait_recv()
        for hh in range(GROUP_HEADS):
            grad_q = pair_terms(g, hh, 0)
            gq_part[0, g, :, part(hh)] = grad_q[:BLOCK]
            gq_part[1, g, :, part(hh)] = grad_q[BLOCK:]

    def work_far(g):
        message(Q3, g).wait_recv()
        for hh in range(GROUP_HEADS):
            grad_q = pair_terms(g, hh, 2)
            gq_part[2, g, :, part(hh)] = grad_q[:BLOCK]
            gq_send[0, g, :, part(hh)] = grad_q[BLOCK:].astype(jnp.bfloat16)

        @pl.when(lands)
        def _():
            leap_gradient(g).start()

        @pl.when(jnp.logical_not(lands))
        def _():
            message(R3, g).start()

        for hh in range(GROUP_HEADS):
            h = g * GROUP_HEADS + hh
            qq = visit[:, g, 0, :, part(hh)].reshape(WINDOW * BLOCK, HEAD_DIM)
            dd = visit[:, g, 1, :, part(hh)].reshape(WINDOW * BLOCK, HEAD_DIM)
            for n, total in ((0, dot(score_grads[h], qq, 1, 0)), (1, dot(probs[h], dd, 1, 0))):
                gkv_near[g, n, :, part(hh)] = total[:BLOCK]
                gkv_send[g, n, :, part(hh)] = total[BLOCK:].astype(jnp.bfloat16)
        message(GKV, g).start()

    def add_second(g):
        @pl.when(skips)
        def _():
            gq_send[1, g] = gq_part[2, g].astype(jnp.bfloat16)

        @pl.when(jnp.logical_not(skips))
        def _():
            message(R3, g).wait_recv()
            total = gq_recv[0, g].astype(jnp.float32) + gq_part[2, g]
            gq_send[1, g] = total.astype(jnp.bfloat16)

        message(R2, g).start()

    def add_first(g):
        message(R2, g).wait_recv()
        total = gq_recv[1, g].astype(jnp.float32) + gq_part[1, g]
        gq_send[2, g] = total.astype(jnp.bfloat16)
        message(R1, g).start()

    def store(n, g):
        out = (gq_out, gk_out, gv_out)[n]
        return pltpu.make_async_copy(done.at[n, g], out.at[:, columns(g)], done_sem.at[n, g])

    def finish(g):
        message(R1, g).wait_recv()
        total = gq_recv[2, g].astype(jnp.float32) + gq_part[0, g]

        @pl.when(leaps)
        def _():
            leap_gradient(g).wait_recv()
            done[0, g] = (total + gq_leap[g].astype(jnp.float32)).astype(jnp.bfloat16)

        @pl.when(jnp.logical_not(leaps))
        def _():
            done[0, g] = total.astype(jnp.bfloat16)

        message(GKV, g).wait_recv()
        for n in range(2):
            total = gkv_near[g, n] + gkv_recv[g, n].astype(jnp.float32)
            done[n + 1, g] = total.astype(jnp.bfloat16)
        for n in range(3):
            store(n, g).start()
        for kind in range(KINDS):
            if kind != Q3:
                message(kind, g).wait_send()

        @pl.when(jnp.logical_not(skips))
        def _():
            message(Q3, g).wait_send()

        @pl.when(leaps)
        def _():
            leap_query(g).wait_send()

    def settle(g):
        for n in range(3):
            store(n, g).wait()

    def at(i, skew, action):
        g = i - skew

        @pl.when((g >= 0) & (g < groups))
        def _():
            action(g)

    def forward_first(g):
        message(Q1, g).wait_recv()
        message(Q2, g).start()

    def forward_second(g):
        message(Q2, g).wait_recv()

        @pl.when(jnp.logical_not(skips))
        def _():
            message(Q3, g).start()

    def stats_forward(w):
        stat_message(w - 1).wait_recv()
        stat_message(w).start()

    def turn(i, carry):
        at(i, -AHEAD, begin_queries)
        at(i, 0, forward_first)

        @pl.when(i == 0)
        def _():
            stats_forward(1)

        at(i, 1, forward_second)

        @pl.when(i == 1)
        def _():
            stats_forward(2)

        at(i, 1, work_near)

        @pl.when(i == 3)
        def _():
            stat_message(2).wait_recv()

        at(i, 3, work_far)
        at(i, 4, add_second)
        at(i, 5, add_first)
        at(i, 6, finish)
        at(i, 7, settle)
        return carry

    for load in loads[:2]:
        load.wait()

    def begin_some_queries(g, carry):
        begin_queries(g)
        return carry

    lax.fori_loop(0, AHEAD, begin_some_queries, 0)
    for load in loads[2:4]:
        load.wait()

    def begin_all_keys(g, carry):
        begin_keys(g)
        return carry

    lax.fori_loop(0, groups, begin_all_keys, 0)
    for load in loads[4:]:
        load.wait()
    make_stats()
    stat_message(0).start()

    lax.fori_loop(0, groups + 7, turn, 0)

    for w in range(WINDOW - 1):
        stat_message(w).wait_send()


def store_kernel(a_ref, b_ref, c_ref, a_out, b_out, c_out, held, in_sem, out_sem):
    half = a_ref.shape[0] // 2
    refs = ((a_ref, a_out), (b_ref, b_out), (c_ref, c_out))
    pieces = [(n, p, pl.ds(p * half, half)) for p in range(2) for n in range(3)]
    fetches = [
        pltpu.make_async_copy(refs[n][0].at[here], held.at[n, here], in_sem.at[n, p])
        for n, p, here in pieces
    ]
    stores = [
        pltpu.make_async_copy(held.at[n, here], refs[n][1].at[here], out_sem.at[n, p])
        for n, p, here in pieces
    ]
    for fetch in fetches:
        fetch.start()
    for fetch, store in zip(fetches, stores):
        fetch.wait()
        store.start()
    for store in stores:
        store.wait()


def local(rows, cols, queries, keys, values, outputs, d_out, row_lse, adjacency):
    tokens, features = queries.shape
    heads = features // HEAD_DIM
    groups = heads // GROUP_HEADS
    width = GROUP_HEADS * HEAD_DIM
    low, wide = jnp.bfloat16, jnp.float32
    hbm = pl.BlockSpec(memory_space=pltpu.HBM)
    out = jax.ShapeDtypeStruct((tokens, features), low)
    pairs = 2 * WINDOW * heads
    grads = pl.pallas_call(
        functools.partial(kernel, rows, cols, groups, heads),
        out_shape=(out, out, out),
        in_specs=[hbm] * 6 + [pl.BlockSpec(memory_space=pltpu.SMEM)],
        out_specs=(hbm, hbm, hbm),
        scratch_shapes=[pltpu.VMEM((tokens, features), low)] * 5
        + [
            pltpu.VMEM((heads, tokens), wide),
            pltpu.SemaphoreType.DMA((8,)),
            pltpu.VMEM((3, groups, BLOCK, width), low),
            pltpu.SemaphoreType.DMA((3, groups)),
            pltpu.VMEM((WINDOW, groups, 2, BLOCK, width), low),
            pltpu.VMEM((groups, 2, 2 * BLOCK, width), low),
            pltpu.VMEM((WINDOW, 2 * heads + 2 * WINDOW, BLOCK), wide),
            pltpu.VMEM((heads, 2 * BLOCK, WINDOW * BLOCK), low),
            pltpu.VMEM((heads, 2 * BLOCK, WINDOW * BLOCK), low),
            pltpu.VMEM((WINDOW - 1, groups, BLOCK, width), wide),
            pltpu.VMEM((groups, 2, BLOCK, width), wide),
            pltpu.VMEM((WINDOW - 1, groups, BLOCK, width), low),
            pltpu.VMEM((WINDOW - 1, groups, BLOCK, width), low),
            pltpu.VMEM((groups, 2, BLOCK, width), low),
            pltpu.VMEM((groups, 2, BLOCK, width), low),
            pltpu.SemaphoreType.DMA((KINDS, groups)),
            pltpu.SemaphoreType.DMA((KINDS, groups)),
            pltpu.SemaphoreType.DMA((WINDOW - 1,)),
            pltpu.SemaphoreType.DMA((WINDOW - 1,)),
            pltpu.VMEM((groups, BLOCK, width), low),
            pltpu.SemaphoreType.DMA((groups,)),
            pltpu.SemaphoreType.DMA((groups,)),
        ],
        compiler_params=pltpu.CompilerParams(
            collective_id=0, has_side_effects=True, vmem_limit_bytes=62 * 1024 * 1024
        ),
        cost_estimate=pl.CostEstimate(
            flops=pairs * 5 * 2 * BLOCK * BLOCK * HEAD_DIM,
            bytes_accessed=8 * tokens * features * 2,
            transcendentals=pairs * BLOCK * BLOCK,
        ),
        name="block_sparse_backward",
    )(queries, keys, values, outputs, d_out, row_lse, adjacency.transpose(0, 1, 3, 2))
    return pl.pallas_call(
        store_kernel,
        out_shape=(out, out, out),
        in_specs=[hbm] * 3,
        out_specs=(hbm, hbm, hbm),
        scratch_shapes=[
            pltpu.VMEM((3, tokens, features), low),
            pltpu.SemaphoreType.DMA((3, 2)),
            pltpu.SemaphoreType.DMA((3, 2)),
        ],
        compiler_params=pltpu.CompilerParams(vmem_limit_bytes=62 * 1024 * 1024),
        name="store_gradients",
    )(*grads)


def solution(mesh):
    token_rows = P(("pb", "ka"), None)
    placed = (token_rows,) * 5 + (P(None, ("pb", "ka")), P(("pb", "ka"), None, None, None))
    return jax.shard_map(
        functools.partial(local, mesh.shape["pb"], mesh.shape["ka"]),
        mesh=mesh,
        in_specs=placed,
        out_specs=(token_rows, token_rows, token_rows),
        check_vma=False,
    )
```

```python
import functools
import math

import jax
import jax.numpy as jnp
from jax import lax
from jax.experimental import pallas as pl
from jax.experimental.pallas import tpu as pltpu
from jax.sharding import PartitionSpec as P

HEAD_DIM = 128
BLOCK = 128
WINDOW = 4
AHEAD = 4
GROUP_HEADS = 2
BIG = 1e30
MESH = pl.DeviceIdType.MESH

Q1, Q2, Q3, KV, R3, R2, R1, GKV = range(8)
KINDS = 8


def dot(a, b, da, db):
    return lax.dot_general(a, b, (((da,), (db,)), ((), ())), preferred_element_type=jnp.float32)


def kernel(
    rows, cols, groups, heads,
    q_hbm, k_hbm, v_hbm, o_hbm, do_hbm, lse_hbm, adj_ref,
    gq_out, gk_out, gv_out,
    q_ref, k_ref, v_ref, o_ref, do_ref, lse_ref, load_sem, done, done_sem,
    visit, kvb, stats, probs, score_grads, gq_part, gkv_near, gq_send, gq_recv, gkv_send, gkv_recv,
    send_sem, recv_sem, stat_send, stat_recv, gq_leap, leap_send, leap_recv,
):
    inverse = 1.0 / math.sqrt(HEAD_DIM)
    width = GROUP_HEADS * HEAD_DIM
    r = lax.axis_index("pb")
    c = lax.axis_index("ka")
    right = (r, lax.rem(c + 1, cols))
    left = (r, lax.rem(c + cols - 1, cols))
    below = (lax.rem(r + 1, rows), c)
    above = (lax.rem(r + rows - 1, rows), c)
    leaps = c == cols - (WINDOW - 1)
    lands = c == 0
    skips = c == cols - 1
    leap_to = (r, 0)
    leap_from = (r, cols - (WINDOW - 1))

    ahead = pl.ds(0, AHEAD * width)
    rest = pl.ds(AHEAD * width, (groups - AHEAD) * width)
    loads = [
        pltpu.make_async_copy(source, target, load_sem.at[n])
        for n, (source, target) in enumerate(
            (
                (q_hbm.at[:, ahead], q_ref.at[:, ahead]),
                (do_hbm.at[:, ahead], do_ref.at[:, ahead]),
                (k_hbm, k_ref),
                (v_hbm, v_ref),
                (q_hbm.at[:, rest], q_ref.at[:, rest]),
                (do_hbm.at[:, rest], do_ref.at[:, rest]),
                (o_hbm, o_ref),
                (lse_hbm, lse_ref),
            )
        )
    ]
    for load in loads:
        load.start()

    barrier = pltpu.get_barrier_semaphore()
    for other in (right, left, below, above):
        pl.semaphore_signal(barrier, inc=1, device_id=other, device_id_type=MESH)

    @pl.when(leaps)
    def _():
        pl.semaphore_signal(barrier, inc=1, device_id=leap_to, device_id_type=MESH)

    @pl.when(lands)
    def _():
        pl.semaphore_signal(barrier, inc=1, device_id=leap_from, device_id_type=MESH)

    @pl.when(leaps | lands)
    def _():
        pl.semaphore_wait(barrier, 5)

    @pl.when(jnp.logical_not(leaps | lands))
    def _():
        pl.semaphore_wait(barrier, 4)

    def message(kind, g):
        if kind in (Q1, Q2, Q3):
            src, dst, to = visit.at[kind, g], visit.at[kind + 1, g], right
        elif kind == KV:
            src = kvb.at[g, :, pl.ds(0, BLOCK), :]
            dst = kvb.at[g, :, pl.ds(BLOCK, BLOCK), :]
            to = above
        elif kind == GKV:
            src, dst, to = gkv_send.at[g], gkv_recv.at[g], below
        else:
            src, dst, to = gq_send.at[kind - R3, g], gq_recv.at[kind - R3, g], left
        return pltpu.make_async_remote_copy(
            src_ref=src, dst_ref=dst,
            send_sem=send_sem.at[kind, g], recv_sem=recv_sem.at[kind, g],
            device_id=to, device_id_type=MESH,
        )

    def leap_query(g):
        return pltpu.make_async_remote_copy(
            src_ref=visit.at[0, g], dst_ref=visit.at[WINDOW - 1, g],
            send_sem=leap_send.at[g], recv_sem=recv_sem.at[Q3, g],
            device_id=leap_to, device_id_type=MESH,
        )

    def leap_gradient(g):
        return pltpu.make_async_remote_copy(
            src_ref=gq_send.at[0, g], dst_ref=gq_leap.at[g],
            send_sem=send_sem.at[R3, g], recv_sem=leap_recv.at[g],
            device_id=leap_from, device_id_type=MESH,
        )

    def stat_message(w):
        return pltpu.make_async_remote_copy(
            src_ref=stats.at[w], dst_ref=stats.at[w + 1],
            send_sem=stat_send.at[w], recv_sem=stat_recv.at[w],
            device_id=right, device_id_type=MESH,
        )

    def columns(g):
        return pl.ds(pl.multiple_of(g * width, width), width)

    def begin_queries(g):
        here = columns(g)
        visit[0, g, 0] = q_ref[:, here]
        visit[0, g, 1] = do_ref[:, here]
        message(Q1, g).start()

        @pl.when(leaps)
        def _():
            leap_query(g).start()

    def begin_keys(g):
        here = columns(g)
        kvb[g, 0, pl.ds(0, BLOCK), :] = k_ref[:, here]
        kvb[g, 1, pl.ds(0, BLOCK), :] = v_ref[:, here]
        message(KV, g).start()

    def make_stats():
        ones = jnp.ones((8, HEAD_DIM), jnp.bfloat16)
        stats[0, pl.ds(0, heads), :] = lse_ref[...]
        for h in range(heads):
            part = pl.ds(h * HEAD_DIM, HEAD_DIM)
            product = do_ref[:, part].astype(jnp.float32) * o_ref[:, part].astype(jnp.float32)
            high = product.astype(jnp.bfloat16)
            low = (product - high.astype(jnp.float32)).astype(jnp.bfloat16)
            delta = dot(ones, high, 1, 1) + dot(ones, low, 1, 1)
            stats[0, pl.ds(heads + h, 1), :] = delta[0:1]
        for a in range(2):
            for w in range(WINDOW):
                blocked = (1 - adj_ref[0, a, 0, w]).astype(jnp.float32) * BIG
                stats[0, pl.ds(2 * heads + a * WINDOW + w, 1), :] = jnp.full((1, BLOCK), blocked, jnp.float32)

    def part(hh):
        return slice(hh * HEAD_DIM, (hh + 1) * HEAD_DIM)

    def pair_terms(g, hh, first):
        h = g * GROUP_HEADS + hh
        pair = (first, first + 1)
        span = pl.ds(first * BLOCK, 2 * BLOCK)
        kk = kvb[g, 0, :, part(hh)]
        vv = kvb[g, 1, :, part(hh)]
        qq = visit[first : first + 2, g, 0, :, part(hh)].reshape(2 * BLOCK, HEAD_DIM)
        dd = visit[first : first + 2, g, 1, :, part(hh)].reshape(2 * BLOCK, HEAD_DIM)
        delta = jnp.concatenate([stats[w, pl.ds(heads + h, 1), :] for w in pair], axis=1)
        for a in range(2):
            norms = jnp.concatenate(
                [
                    stats[w, pl.ds(h, 1), :] + stats[w, pl.ds(2 * heads + a * WINDOW + w, 1), :]
                    for w in pair
                ],
                axis=1,
            )
            half = slice(a * BLOCK, (a + 1) * BLOCK)
            prob = jnp.exp(dot(kk[half], qq, 1, 1) * inverse - norms)
            probs[h, half, span] = prob.astype(jnp.bfloat16)
            prob_grad = dot(vv[half], dd, 1, 1)
            score_grad = prob * (prob_grad - delta) * inverse
            score_grads[h, half, span] = score_grad.astype(jnp.bfloat16)
        return dot(score_grads[h, :, span], kk, 0, 0)

    def work_near(g):
        message(KV, g).wait_recv()
        for hh in range(GROUP_HEADS):
            grad_q = pair_terms(g, hh, 0)
            gq_part[0, g, :, part(hh)] = grad_q[:BLOCK]
            gq_part[1, g, :, part(hh)] = grad_q[BLOCK:]

    def work_far(g):
        message(Q3, g).wait_recv()
        for hh in range(GROUP_HEADS):
            grad_q = pair_terms(g, hh, 2)
            gq_part[2, g, :, part(hh)] = grad_q[:BLOCK]
            gq_send[0, g, :, part(hh)] = grad_q[BLOCK:].astype(jnp.bfloat16)

        @pl.when(lands)
        def _():
            leap_gradient(g).start()

        @pl.when(jnp.logical_not(lands))
        def _():
            message(R3, g).start()

        for hh in range(GROUP_HEADS):
            h = g * GROUP_HEADS + hh
            qq = visit[:, g, 0, :, part(hh)].reshape(WINDOW * BLOCK, HEAD_DIM)
            dd = visit[:, g, 1, :, part(hh)].reshape(WINDOW * BLOCK, HEAD_DIM)
            for n, total in ((0, dot(score_grads[h], qq, 1, 0)), (1, dot(probs[h], dd, 1, 0))):
                gkv_near[g, n, :, part(hh)] = total[:BLOCK]
                gkv_send[g, n, :, part(hh)] = total[BLOCK:].astype(jnp.bfloat16)
        message(GKV, g).start()

    def add_second(g):
        @pl.when(skips)
        def _():
            gq_send[1, g] = gq_part[2, g].astype(jnp.bfloat16)

        @pl.when(jnp.logical_not(skips))
        def _():
            message(R3, g).wait_recv()
            total = gq_recv[0, g].astype(jnp.float32) + gq_part[2, g]
            gq_send[1, g] = total.astype(jnp.bfloat16)

        message(R2, g).start()

    def add_first(g):
        message(R2, g).wait_recv()
        total = gq_recv[1, g].astype(jnp.float32) + gq_part[1, g]
        gq_send[2, g] = total.astype(jnp.bfloat16)
        message(R1, g).start()

    def store(n, g):
        out = (gq_out, gk_out, gv_out)[n]
        return pltpu.make_async_copy(done.at[n, g], out.at[:, columns(g)], done_sem.at[n, g])

    def finish(g):
        message(R1, g).wait_recv()
        total = gq_recv[2, g].astype(jnp.float32) + gq_part[0, g]

        @pl.when(leaps)
        def _():
            leap_gradient(g).wait_recv()
            done[0, g] = (total + gq_leap[g].astype(jnp.float32)).astype(jnp.bfloat16)

        @pl.when(jnp.logical_not(leaps))
        def _():
            done[0, g] = total.astype(jnp.bfloat16)

        message(GKV, g).wait_recv()
        for n in range(2):
            total = gkv_near[g, n] + gkv_recv[g, n].astype(jnp.float32)
            done[n + 1, g] = total.astype(jnp.bfloat16)
        for n in range(3):
            store(n, g).start()
        for kind in range(KINDS):
            if kind != Q3:
                message(kind, g).wait_send()

        @pl.when(jnp.logical_not(skips))
        def _():
            message(Q3, g).wait_send()

        @pl.when(leaps)
        def _():
            leap_query(g).wait_send()

    def settle(g):
        for n in range(3):
            store(n, g).wait()

    def at(i, skew, action):
        g = i - skew

        @pl.when((g >= 0) & (g < groups))
        def _():
            action(g)

    def forward_first(g):
        message(Q1, g).wait_recv()
        message(Q2, g).start()

    def forward_second(g):
        message(Q2, g).wait_recv()

        @pl.when(jnp.logical_not(skips))
        def _():
            message(Q3, g).start()

    def stats_forward(w):
        stat_message(w - 1).wait_recv()
        stat_message(w).start()

    def turn(i, carry):
        at(i, -AHEAD, begin_queries)
        at(i, 0, forward_first)

        @pl.when(i == 0)
        def _():
            stats_forward(1)

        at(i, 1, forward_second)

        @pl.when(i == 1)
        def _():
            stats_forward(2)

        at(i, 1, work_near)

        @pl.when(i == 2)
        def _():
            stat_message(2).wait_recv()

        at(i, 2, work_far)
        at(i, 3, add_second)
        at(i, 4, add_first)
        at(i, 5, finish)
        at(i, 6, settle)
        return carry

    for load in loads[:2]:
        load.wait()

    def begin_some_queries(g, carry):
        begin_queries(g)
        return carry

    lax.fori_loop(0, AHEAD, begin_some_queries, 0)
    for load in loads[2:4]:
        load.wait()

    def begin_all_keys(g, carry):
        begin_keys(g)
        return carry

    lax.fori_loop(0, groups, begin_all_keys, 0)
    for load in loads[4:]:
        load.wait()
    make_stats()
    stat_message(0).start()

    lax.fori_loop(0, groups + 6, turn, 0)

    for w in range(WINDOW - 1):
        stat_message(w).wait_send()


def store_kernel(a_ref, b_ref, c_ref, a_out, b_out, c_out, held, in_sem, out_sem):
    half = a_ref.shape[0] // 2
    refs = ((a_ref, a_out), (b_ref, b_out), (c_ref, c_out))
    pieces = [(n, p, pl.ds(p * half, half)) for p in range(2) for n in range(3)]
    fetches = [
        pltpu.make_async_copy(refs[n][0].at[here], held.at[n, here], in_sem.at[n, p])
        for n, p, here in pieces
    ]
    stores = [
        pltpu.make_async_copy(held.at[n, here], refs[n][1].at[here], out_sem.at[n, p])
        for n, p, here in pieces
    ]
    for fetch in fetches:
        fetch.start()
    for fetch, store in zip(fetches, stores):
        fetch.wait()
        store.start()
    for store in stores:
        store.wait()


def local(rows, cols, queries, keys, values, outputs, d_out, row_lse, adjacency):
    tokens, features = queries.shape
    heads = features // HEAD_DIM
    groups = heads // GROUP_HEADS
    width = GROUP_HEADS * HEAD_DIM
    low, wide = jnp.bfloat16, jnp.float32
    hbm = pl.BlockSpec(memory_space=pltpu.HBM)
    out = jax.ShapeDtypeStruct((tokens, features), low)
    pairs = 2 * WINDOW * heads
    grads = pl.pallas_call(
        functools.partial(kernel, rows, cols, groups, heads),
        out_shape=(out, out, out),
        in_specs=[hbm] * 6 + [pl.BlockSpec(memory_space=pltpu.SMEM)],
        out_specs=(hbm, hbm, hbm),
        scratch_shapes=[pltpu.VMEM((tokens, features), low)] * 5
        + [
            pltpu.VMEM((heads, tokens), wide),
            pltpu.SemaphoreType.DMA((8,)),
            pltpu.VMEM((3, groups, BLOCK, width), low),
            pltpu.SemaphoreType.DMA((3, groups)),
            pltpu.VMEM((WINDOW, groups, 2, BLOCK, width), low),
            pltpu.VMEM((groups, 2, 2 * BLOCK, width), low),
            pltpu.VMEM((WINDOW, 2 * heads + 2 * WINDOW, BLOCK), wide),
            pltpu.VMEM((heads, 2 * BLOCK, WINDOW * BLOCK), low),
            pltpu.VMEM((heads, 2 * BLOCK, WINDOW * BLOCK), low),
            pltpu.VMEM((WINDOW - 1, groups, BLOCK, width), wide),
            pltpu.VMEM((groups, 2, BLOCK, width), wide),
            pltpu.VMEM((WINDOW - 1, groups, BLOCK, width), low),
            pltpu.VMEM((WINDOW - 1, groups, BLOCK, width), low),
            pltpu.VMEM((groups, 2, BLOCK, width), low),
            pltpu.VMEM((groups, 2, BLOCK, width), low),
            pltpu.SemaphoreType.DMA((KINDS, groups)),
            pltpu.SemaphoreType.DMA((KINDS, groups)),
            pltpu.SemaphoreType.DMA((WINDOW - 1,)),
            pltpu.SemaphoreType.DMA((WINDOW - 1,)),
            pltpu.VMEM((groups, BLOCK, width), low),
            pltpu.SemaphoreType.DMA((groups,)),
            pltpu.SemaphoreType.DMA((groups,)),
        ],
        compiler_params=pltpu.CompilerParams(
            collective_id=0, has_side_effects=True, vmem_limit_bytes=62 * 1024 * 1024
        ),
        cost_estimate=pl.CostEstimate(
            flops=pairs * 5 * 2 * BLOCK * BLOCK * HEAD_DIM,
            bytes_accessed=8 * tokens * features * 2,
            transcendentals=pairs * BLOCK * BLOCK,
        ),
        name="block_sparse_backward",
    )(queries, keys, values, outputs, d_out, row_lse, adjacency.transpose(0, 1, 3, 2))
    return pl.pallas_call(
        store_kernel,
        out_shape=(out, out, out),
        in_specs=[hbm] * 3,
        out_specs=(hbm, hbm, hbm),
        scratch_shapes=[
            pltpu.VMEM((3, tokens, features), low),
            pltpu.SemaphoreType.DMA((3, 2)),
            pltpu.SemaphoreType.DMA((3, 2)),
        ],
        compiler_params=pltpu.CompilerParams(vmem_limit_bytes=62 * 1024 * 1024),
        name="store_gradients",
    )(*grads)


def solution(mesh):
    token_rows = P(("pb", "ka"), None)
    placed = (token_rows,) * 5 + (P(None, ("pb", "ka")), P(("pb", "ka"), None, None, None))
    return jax.shard_map(
        functools.partial(local, mesh.shape["pb"], mesh.shape["ka"]),
        mesh=mesh,
        in_specs=placed,
        out_specs=(token_rows, token_rows, token_rows),
        check_vma=False,
    )
```
